512 devices in a mesh: dp: 8 (over x, core), fsdp: 4 (over y), seq: 16 (over z).
Axes of the slice: x: 4, y: 4, z: 16, core: 2. Of those that a mesh axis runs over, the one named last changes fastest.
Arguments:
- query_states: bfloat16 [32, 16, 128, 1536], P(('dp', 'fsdp'), 'seq'), may hold values from -8 to 8
- key_states: bfloat16 [32, 16, 128, 1536], P(('dp', 'fsdp'), 'seq'), may hold values from -8 to 8
- value_states: bfloat16 [32, 16, 128, 1536], P(('dp', 'fsdp'), 'seq'), may hold values from -6 to 6
- out_weight: bfloat16 [1536, 1536], P(('fsdp', 'seq')), may hold values from -0.15625 to 0.15625
- gate_space: float32 [1536], replicated, may hold values from -4 to 4
- gate_time: float32 [1536], replicated, may hold values from -4 to 4
- upstream: bfloat16 [32, 16, 128, 1536], P(('dp', 'fsdp'), 'seq'), may hold values from -6 to 6
- frame_count: int32 [32], P(('dp', 'fsdp')), may hold values from 4 to 16, as said below
- pos_count: int32 [32], P(('dp', 'fsdp')), may hold values from 32 to 128, as said below
Outputs:
- output_states: bfloat16 [32, 16, 128, 1536], P(('dp', 'fsdp'), 'seq')
- grad_query: bfloat16 [32, 16, 128, 1536], P(('dp', 'fsdp'), 'seq')
- grad_key: bfloat16 [32, 16, 128, 1536], P(('dp', 'fsdp'), 'seq')
- grad_value: bfloat16 [32, 16, 128, 1536], P(('dp', 'fsdp'), 'seq')
- grad_gate_space: float32 [1536], replicated
- grad_gate_time: float32 [1536], replicated
The draws below stay inside these ranges and needn't reach their ends.
Inputs may be any that keep to these rules, and one draw needn't show every extreme that they name: `frame_count`: in every draw some clip has all 16 frames valid. `pos_count`: in every draw some clip has all 128 positions valid.
All inputs are finite; a program needn't handle non-finite values.
Results may differ from the reference program's by a relative error of at most 0.012.
Values may be sent and summed in bfloat16 or wider, within the bound.
No kernel may reach another device: no remote copies, remote signals or barrier semaphores. Data moves between devices by JAX's collectives and lax.ppermute only.
A program may use at most 64 MiB of HBM per device.

```python
import jax
import jax.numpy as jnp
from jax import lax

HEAD = 128
POS = 128
CHANNELS = 1536
FRAMES = 16
GROUPS = 32


def mixed_draw(own):
    drawn = jnp.clip(jax.random.normal(own, (GROUPS, FRAMES, POS, CHANNELS)), -6.0, 6.0)
    return drawn.astype(jnp.bfloat16)


def draw_query_states(key, part):
    own = jax.random.fold_in(key, 21)
    return mixed_draw(own)


def draw_key_states(key, part):
    own = jax.random.fold_in(key, 22)
    return mixed_draw(own)


def draw_frame_count(key, part):
    key = jax.random.fold_in(key, 11)
    first, second = jax.random.split(key)
    counts = jax.random.randint(first, (GROUPS,), max(1, FRAMES // 4), FRAMES + 1)
    where = jax.random.randint(second, (), 0, GROUPS)
    return jnp.where(jnp.arange(GROUPS) == where, FRAMES, counts).astype(jnp.int32)


def draw_pos_count(key, part):
    key = jax.random.fold_in(key, 12)
    first, second = jax.random.split(key)
    counts = jax.random.randint(first, (GROUPS,), POS // 4, POS + 1)
    where = jax.random.randint(second, (), 0, GROUPS)
    return jnp.where(jnp.arange(GROUPS) == where, POS, counts).astype(jnp.int32)


def steps_of(rng, extent, shards, least, top_value):
    loudness, own = 1.0, jax.random.fold_in(rng, 6)
    for position, blocks in shards:
        steps = jnp.exp(jax.random.uniform(jax.random.fold_in(own, position), (blocks,), jnp.float32, least / len(shards), top_value / len(shards)))
        loudness = loudness * jnp.repeat(steps, extent[position] // blocks).reshape([-1 if axis == position else 1 for axis in range(len(extent))])
    return loudness


def scatter_about(stream_key, extent, deviation, reach, shards=(), held_as=jnp.bfloat16):
    gain = steps_of(stream_key, extent, shards, -0.22, 0.18) if shards else 1.0
    drawn = jax.random.normal(stream_key, extent, jnp.float32) * deviation * gain
    return jnp.minimum(jnp.maximum(drawn, -reach), reach).astype(held_as)


def setup_inputs(seed: int = 0) -> dict:
    splits = jax.random.split(jax.random.key(seed), 10)
    query_states = draw_query_states(jax.random.fold_in(splits[9], 71), 0)
    key_states = draw_key_states(jax.random.fold_in(splits[9], 71), 0)
    value_states = scatter_about(splits[2], (GROUPS, FRAMES, POS, CHANNELS), 1.0, 6.0, ((0, 32), (1, 16)))
    out_weight = scatter_about(splits[3], (CHANNELS, CHANNELS), CHANNELS ** -0.5, 0.15625, ((0, 64),))
    gate_space = scatter_about(splits[4], (CHANNELS,), 1.0, 4.0, (), jnp.float32)
    gate_time = scatter_about(splits[5], (CHANNELS,), 1.0, 4.0, (), jnp.float32)
    upstream = scatter_about(splits[6], (GROUPS, FRAMES, POS, CHANNELS), 1.0, 6.0, ((0, 32), (1, 16)))
    frame_count = draw_frame_count(jax.random.fold_in(splits[9], 71), 0)
    pos_count = draw_pos_count(jax.random.fold_in(splits[9], 71), 0)
    return {"query_states": query_states, "key_states": key_states, "value_states": value_states, "out_weight": out_weight, "gate_space": gate_space, "gate_time": gate_time, "upstream": upstream, "frame_count": frame_count, "pos_count": pos_count}


NEGATIVE = -1e+30

def other_form(form):
    return form.replace('l', 'm')

def softmax_rows(scores, keep):
    masked = jnp.where(keep, scores, NEGATIVE)
    highest = lax.optimization_barrier(jnp.max(masked, axis=-1, keepdims=True))
    raised = jnp.exp(masked - highest)
    return raised / lax.optimization_barrier(jnp.sum(raised, axis=-1, keepdims=True))

def attention_scores(queries, keys, form):
    scale = queries.shape[-1] ** (-0.5)
    return jnp.einsum(form + ',' + other_form(form) + '->bhlm', queries.astype(jnp.float32), keys.astype(jnp.float32)) * scale

def attend(queries, keys, values, keep, form):
    probs = softmax_rows(attention_scores(queries, keys, form), keep).astype(jnp.bfloat16)
    result = jnp.einsum('bhlm,' + other_form(form) + '->' + form, probs.astype(jnp.float32), values.astype(jnp.float32))
    return result.astype(jnp.bfloat16)

def attend_grad(queries, keys, values, keep, form, incoming):
    scale = queries.shape[-1] ** (-0.5)
    other = other_form(form)
    probs = softmax_rows(attention_scores(queries, keys, form), keep)
    rounded = probs.astype(jnp.bfloat16).astype(jnp.float32)
    grad_values = jnp.einsum('bhlm,' + form + '->' + other, rounded, incoming.astype(jnp.float32))
    grad_probs = jnp.einsum(form + ',' + other + '->bhlm', incoming.astype(jnp.float32), values.astype(jnp.float32))
    inner = lax.optimization_barrier(jnp.sum(probs * grad_probs, axis=-1, keepdims=True))
    grad_scores = (probs * (grad_probs - inner) * scale).astype(jnp.bfloat16).astype(jnp.float32)
    grad_queries = jnp.einsum('bhlm,' + other + '->' + form, grad_scores, keys.astype(jnp.float32))
    grad_keys = jnp.einsum('bhlm,' + form + '->' + other, grad_scores, queries.astype(jnp.float32))
    return (grad_queries, grad_keys, grad_values)

def reference(query_states, key_states, value_states, out_weight, gate_space, gate_time, upstream, frame_count, pos_count):

    def one_group(items):
        queries, keys, values, incoming, frame_total, pos_total = items
        frames, positions, channels = queries.shape
        heads = channels // HEAD

        def split(array):
            return array.reshape(frames, positions, heads, HEAD)
        keep_space = (jnp.arange(positions) < pos_total)[None, None, None, :]
        keep_time = (jnp.arange(frames) < frame_total)[None, None, None, :]
        spatial = attend(split(queries), split(keys), split(values), keep_space, 'blhe').reshape(frames * positions, channels)
        temporal = attend(split(queries), split(keys), split(values), keep_time, 'lbhe').reshape(frames * positions, channels)
        mixed = (gate_space * spatial.astype(jnp.float32) + gate_time * temporal.astype(jnp.float32)).astype(jnp.bfloat16)
        output = jnp.dot(mixed, out_weight, preferred_element_type=jnp.float32).astype(jnp.bfloat16)
        flat_up = incoming.reshape(frames * positions, channels)
        grad_mixed = jnp.dot(flat_up, out_weight.T, preferred_element_type=jnp.float32)
        part_space = lax.optimization_barrier(jnp.sum(grad_mixed * spatial.astype(jnp.float32), axis=0))
        part_time = lax.optimization_barrier(jnp.sum(grad_mixed * temporal.astype(jnp.float32), axis=0))
        down_space = (gate_space * grad_mixed).astype(jnp.bfloat16)
        down_time = (gate_time * grad_mixed).astype(jnp.bfloat16)
        space_grads = attend_grad(split(queries), split(keys), split(values), keep_space, 'blhe', split(down_space))
        time_grads = attend_grad(split(queries), split(keys), split(values), keep_time, 'lbhe', split(down_time))

        def combine(local, moved):
            moved = lax.optimization_barrier(moved.astype(jnp.bfloat16))
            return (local + moved.astype(jnp.float32)).astype(jnp.bfloat16).reshape(frames, positions, channels)
        return (output.reshape(frames, positions, channels), combine(space_grads[0], time_grads[0]), combine(space_grads[1], time_grads[1]), combine(space_grads[2], time_grads[2]), part_space, part_time)
    results = lax.map(one_group, (query_states, key_states, value_states, upstream, frame_count, pos_count))
    total = jnp.sqrt(jnp.float32(GROUPS * FRAMES * POS))
    return (results[0], results[1], results[2], results[3], lax.optimization_barrier(jnp.sum(results[4], axis=0)) / total, lax.optimization_barrier(jnp.sum(results[5], axis=0)) / total)
```

```python
import functools
import math

import jax
import jax.numpy as jnp
from jax import lax
from jax.experimental import pallas as pl
from jax.experimental.pallas import tpu as pltpu
from jax.sharding import Mesh, PartitionSpec as P

HEAD = 128
NEGATIVE = -1e30
VMEM_BYTES = 48 * 1024 * 1024
ROWS = 8
PIECES = 5


def contract(left, right, left_dim, right_dim):
    return lax.dot_general(
        left,
        right,
        (((left_dim,), (right_dim,)), ((), ())),
        preferred_element_type=jnp.float32,
    )


def head_gradients(query, key, value, grad_mixed, gate, keep):
    scale = HEAD ** (-0.5)
    incoming = (gate * grad_mixed).astype(jnp.bfloat16)
    scores = jnp.where(keep, contract(key, query, 1, 1) * scale, NEGATIVE)
    raised = jnp.exp(scores - jnp.max(scores, axis=0, keepdims=True))
    probs = raised / jnp.sum(raised, axis=0, keepdims=True)
    rounded = probs.astype(jnp.bfloat16)
    result = contract(rounded, value, 0, 0).astype(jnp.bfloat16)
    part = jnp.sum(grad_mixed * result.astype(jnp.float32), axis=0, keepdims=True)
    grad_value = contract(rounded, incoming, 1, 0)
    grad_probs = contract(value, incoming, 1, 1)
    inner = jnp.sum(probs * grad_probs, axis=0, keepdims=True)
    grad_scores = (probs * (grad_probs - inner) * scale).astype(jnp.bfloat16)
    grad_query = contract(grad_scores, key, 0, 0)
    grad_key = contract(grad_scores, query, 1, 0)
    return result, grad_query, grad_key, grad_value, part


def time_kernel(count_ref, moved_ref, mixed_ref, gate_ref, out_ref, part_ref):
    frames, _, near, channels = moved_ref.shape
    tokens = frames * near
    key_at = lax.broadcasted_iota(jnp.int32, (tokens, tokens), 0)
    query_at = lax.broadcasted_iota(jnp.int32, (tokens, tokens), 1)
    keep = (key_at % near == query_at % near) & (key_at < count_ref[0] * near)
    for head in range(channels // HEAD):
        lanes = slice(head * HEAD, (head + 1) * HEAD)

        def load(which):
            wide = moved_ref[:, which, :, lanes].astype(jnp.float32)
            return wide.reshape(tokens, HEAD).astype(jnp.bfloat16)

        result, grad_query, grad_key, grad_value, part = head_gradients(
            load(0), load(1), load(2), mixed_ref[:, lanes], gate_ref[:, lanes], keep
        )
        part_ref[:, lanes] = part
        for which, array in enumerate((result, grad_query, grad_key, grad_value)):
            wide = array.astype(jnp.float32).reshape(frames, near, HEAD)
            out_ref[:, which, :, lanes] = wide.astype(jnp.bfloat16)


def space_kernel(
    count_ref, query_ref, key_ref, value_ref, mixed_ref, gate_ref,
    out_ref, grad_query_ref, grad_key_ref, grad_value_ref, part_ref,
):
    tokens, channels = query_ref.shape
    keep = lax.broadcasted_iota(jnp.int32, (tokens, tokens), 0) < count_ref[0]
    for head in range(channels // HEAD):
        lanes = slice(head * HEAD, (head + 1) * HEAD)
        result, grad_query, grad_key, grad_value, part = head_gradients(
            query_ref[:, lanes], key_ref[:, lanes], value_ref[:, lanes],
            mixed_ref[:, lanes], gate_ref[:, lanes], keep,
        )
        out_ref[:, lanes] = result
        grad_query_ref[:, lanes] = grad_query
        grad_key_ref[:, lanes] = grad_key
        grad_value_ref[:, lanes] = grad_value
        part_ref[:, lanes] = part


def in_vmem(count):
    return [pl.BlockSpec(memory_space=pltpu.VMEM)] * count


def attention_cost(tokens, channels):
    return pl.CostEstimate(
        flops=12 * tokens * tokens * channels,
        bytes_accessed=16 * tokens * channels,
        transcendentals=tokens * tokens * channels // HEAD,
    )


def time_attention(count, moved, grad_mixed, gate):
    frames, _, near, channels = moved.shape
    return pl.pallas_call(
        time_kernel,
        out_shape=(
            jax.ShapeDtypeStruct((frames, 4, near, channels), jnp.bfloat16),
            jax.ShapeDtypeStruct((1, channels), jnp.float32),
        ),
        in_specs=[pl.BlockSpec(memory_space=pltpu.SMEM)] + in_vmem(3),
        out_specs=tuple(in_vmem(2)),
        cost_estimate=attention_cost(frames * near, channels),
        compiler_params=pltpu.CompilerParams(vmem_limit_bytes=VMEM_BYTES),
        name="time_attention",
    )(count, moved, grad_mixed, gate)


def space_attention(count, query, key, value, grad_mixed, gate):
    tokens, channels = query.shape
    wide = jax.ShapeDtypeStruct((tokens, channels), jnp.float32)
    return pl.pallas_call(
        space_kernel,
        out_shape=(
            jax.ShapeDtypeStruct((tokens, channels), jnp.bfloat16),
            wide, wide, wide,
            jax.ShapeDtypeStruct((1, channels), jnp.float32),
        ),
        in_specs=[pl.BlockSpec(memory_space=pltpu.SMEM)] + in_vmem(5),
        out_specs=tuple(in_vmem(5)),
        cost_estimate=attention_cost(tokens, channels),
        compiler_params=pltpu.CompilerParams(vmem_limit_bytes=VMEM_BYTES),
        name="space_attention",
    )(count, query, key, value, grad_mixed, gate)


def tail_kernel(
    time_ref, moved_query_ref, moved_key_ref, moved_value_ref, space_ref,
    grad_query_ref, grad_key_ref, grad_value_ref, gate_space_ref, gate_time_ref, weight_ref,
    out_ref, out_query_ref, out_key_ref, out_value_ref, mixed_ref,
):
    tokens, columns = grad_query_ref.shape

    @pl.when(pl.program_id(0) == 0)
    def _():
        moved = time_ref[...].astype(jnp.float32).reshape(space_ref.shape)
        space = space_ref[...].astype(jnp.float32)
        mixed_ref[...] = (gate_space_ref[...] * space + gate_time_ref[...] * moved).astype(jnp.bfloat16)

    out_ref[...] = contract(mixed_ref[...], weight_ref[...], 1, 0).astype(jnp.bfloat16)
    for target, local, moved in (
        (out_query_ref, grad_query_ref, moved_query_ref),
        (out_key_ref, grad_key_ref, moved_key_ref),
        (out_value_ref, grad_value_ref, moved_value_ref),
    ):
        wide = moved[...].astype(jnp.float32).reshape(tokens, columns)
        target[...] = (local[...] + wide).astype(jnp.bfloat16)


def tail(returned, space, space_grads, gate_space, gate_time, weight, block=256):
    owners, _, near, channels = returned.shape
    tokens = owners * near

    def moved(which):
        return pl.BlockSpec((owners, 1, near, block), lambda j: (0, which, 0, j))

    whole = pl.BlockSpec((tokens, channels), lambda j: (0, 0))
    columns = pl.BlockSpec((tokens, block), lambda j: (0, j))
    gate = pl.BlockSpec((1, channels), lambda j: (0, 0))
    return pl.pallas_call(
        tail_kernel,
        grid=(channels // block,),
        out_shape=(jax.ShapeDtypeStruct((tokens, channels), jnp.bfloat16),) * 4,
        in_specs=[
            pl.BlockSpec((owners, 1, near, channels), lambda j: (0, 0, 0, 0)),
            moved(1), moved(2), moved(3), whole, columns, columns, columns, gate, gate,
            pl.BlockSpec((channels, block), lambda j: (0, j)),
        ],
        out_specs=(columns,) * 4,
        scratch_shapes=[pltpu.VMEM((tokens, channels), jnp.bfloat16)],
        compiler_params=pltpu.CompilerParams(vmem_limit_bytes=VMEM_BYTES),
        name="tail",
    )(returned, returned, returned, returned, space, *space_grads, gate_space, gate_time, weight)


def ring_of_four(block, axis):
    def shift(array, by):
        return lax.ppermute(array, axis, [(i, (i + by) % 4) for i in range(4)])

    half = block.shape[0] // 2
    before, after = shift(block, 1), shift(block, -1)
    across = jnp.concatenate([shift(before[:half], 1), shift(after[half:], -1)], axis=0)
    ring = jnp.stack([block, after, across, before] * 2)
    start = (4 - lax.axis_index(axis)) % 4
    return lax.dynamic_slice_in_dim(ring, start, 4, axis=0)


def own_pieces(out_weight):
    rows, channels = out_weight.shape
    wide = channels // lax.axis_size("x")
    block = lax.dynamic_slice_in_dim(out_weight, lax.axis_index("x") * wide, wide, axis=1)
    side = block.reshape(rows // ROWS, ROWS, wide).transpose(1, 0, 2).reshape(ROWS, rows * wide // ROWS)
    start = lax.axis_index("core") * (PIECES - 1) * HEAD
    return lax.dynamic_slice_in_dim(side, start, PIECES * HEAD, axis=1)


def whole_weight(pieces, rows, channels):
    seq = pieces.shape[0]
    along_y = ring_of_four(pieces, "fsdp")
    along_x = ring_of_four(along_y.reshape(4 * seq, ROWS, PIECES * HEAD), "x")
    other = lax.ppermute(along_x, "core", [(0, 1), (1, 0)])
    first = lax.axis_index("core") == 0
    low, high = jnp.where(first, along_x, other), jnp.where(first, other, along_x)
    side = jnp.concatenate([low, high[..., HEAD:]], axis=-1)
    wide = channels // 4
    side = side.reshape(4, 4 * seq, ROWS, rows // ROWS, wide)
    return side.transpose(1, 3, 2, 0, 4).reshape(channels, channels)


def all_sum(array, axis):
    return jnp.sum(lax.all_gather(array, axis, axis=0, tiled=True), axis=0, keepdims=True)


def on_device(
    query_states,
    key_states,
    value_states,
    out_weight,
    gate_space,
    gate_time,
    upstream,
    frame_count,
    pos_count,
):
    _, frames_here, positions, channels = query_states.shape
    owners = lax.axis_size("seq")
    near = positions // owners
    rows = out_weight.shape[0]
    gate_space, gate_time = gate_space.reshape(1, channels), gate_time.reshape(1, channels)
    query, key, value, flat_up = (
        array.reshape(positions, channels)
        for array in (query_states, key_states, value_states, upstream)
    )

    def exchange(array):
        return lax.all_to_all(array, "seq", split_axis=0, concat_axis=0, tiled=True)

    pieces = jnp.broadcast_to(own_pieces(out_weight), (owners, ROWS, PIECES * HEAD))
    first = exchange(jnp.concatenate([flat_up.reshape(owners, near, channels), pieces], axis=-1))
    second = jnp.stack([array.reshape(owners, near, channels) for array in (query, key, value)], axis=1)
    first, second = lax.optimization_barrier((first, second))
    moved = exchange(second)

    weight = whole_weight(first[..., channels:], rows, channels)
    both = jnp.concatenate([flat_up, first[..., :channels].reshape(positions, channels)], axis=0)
    grad_mixed = jnp.einsum("td,nd->tn", both, weight, preferred_element_type=jnp.float32)
    here, there = grad_mixed[:positions], grad_mixed[positions:]

    back, part_time = time_attention(frame_count, moved, there, gate_time)
    returned = exchange(back)

    space, *space_grads, part_space = space_attention(pos_count, query, key, value, here, gate_space)
    parts = jnp.concatenate([part_space, part_time], axis=1)
    for axis in (("x", "core"), "fsdp", "seq"):
        parts = all_sum(parts, axis)
    tokens = lax.axis_size("x") * lax.axis_size("core") * lax.axis_size("fsdp") * owners * frames_here * positions
    totals = parts[0] / math.sqrt(tokens)

    results = tail(returned, space, space_grads, gate_space, gate_time, weight)
    shaped = tuple(array.reshape(query_states.shape) for array in results)
    return shaped + (totals[:channels], totals[channels:])


def solution(mesh):
    chips = mesh.shape["dp"] // 2
    split = Mesh(
        mesh.devices.reshape(chips, 2, mesh.shape["fsdp"], mesh.shape["seq"]),
        ("x", "core", "fsdp", "seq"),
    )
    clips = ("x", "core", "fsdp")
    states = P(clips, "seq", None, None)
    return jax.shard_map(
        on_device,
        mesh=split,
        in_specs=(states, states, states, P(("fsdp", "seq"), None), P(), P(), states, P(clips), P(clips)),
        out_specs=(states, states, states, states, P(), P()),
        check_vma=False,
    )
```

```python
import functools
import math

import jax
import jax.numpy as jnp
from jax import lax
from jax.experimental import pallas as pl
from jax.experimental.pallas import tpu as pltpu
from jax.sharding import Mesh, PartitionSpec as P

HEAD = 128
NEGATIVE = -1e30
VMEM_BYTES = 20 * 1024 * 1024
DISTANCES = (((0, 8), (4, -4)), ((1, -1), (7, -7)), ((2, -2), (6, -6)), ((3, -3), (5, -5)))


def contract(left, right, left_dim, right_dim):
    return lax.dot_general(
        left,
        right,
        (((left_dim,), (right_dim,)), ((), ())),
        preferred_element_type=jnp.float32,
    )


def head_gradients(query, key, value, grad_mixed, gate, keep):
    scale = HEAD ** (-0.5)
    incoming = (gate * grad_mixed).astype(jnp.bfloat16)
    scores = jnp.where(keep, contract(key, query, 1, 1) * scale, NEGATIVE)
    raised = jnp.exp(scores - jnp.max(scores, axis=0, keepdims=True))
    probs = raised / jnp.sum(raised, axis=0, keepdims=True)
    rounded = probs.astype(jnp.bfloat16)
    result = contract(rounded, value, 0, 0).astype(jnp.bfloat16)
    part = jnp.sum(grad_mixed * result.astype(jnp.float32), axis=0, keepdims=True)
    grad_value = contract(rounded, incoming, 1, 0)
    grad_probs = contract(value, incoming, 1, 1)
    inner = jnp.sum(probs * grad_probs, axis=0, keepdims=True)
    grad_scores = (probs * (grad_probs - inner) * scale).astype(jnp.bfloat16)
    grad_query = contract(grad_scores, key, 0, 0)
    grad_key = contract(grad_scores, query, 1, 0)
    return result, grad_query, grad_key, grad_value, part


def time_kernel(count_ref, moved_ref, mixed_ref, gate_ref, out_ref, grad_ref, part_ref):
    frames, _, near, channels = moved_ref.shape
    tokens = frames * near
    key_at = lax.broadcasted_iota(jnp.int32, (tokens, tokens), 0)
    query_at = lax.broadcasted_iota(jnp.int32, (tokens, tokens), 1)
    keep = (key_at % near == query_at % near) & (key_at < count_ref[0] * near)
    for head in range(channels // HEAD):
        lanes = slice(head * HEAD, (head + 1) * HEAD)

        def load(which):
            wide = moved_ref[:, which, :, lanes].astype(jnp.float32)
            return wide.reshape(tokens, HEAD).astype(jnp.bfloat16)

        result, grad_query, grad_key, grad_value, part = head_gradients(
            load(0), load(1), load(2), mixed_ref[:, lanes], gate_ref[:, lanes], keep
        )
        part_ref[:, lanes] = part
        for target, which, array in (
            (out_ref, 0, result), (out_ref, 1, grad_query), (grad_ref, 0, grad_key), (grad_ref, 1, grad_value),
        ):
            wide = array.astype(jnp.float32).reshape(frames, near, HEAD)
            target[:, which, :, lanes] = wide.astype(jnp.bfloat16)


def space_kernel(
    count_ref, query_ref, key_ref, value_ref, mixed_ref, gate_ref,
    out_ref, grad_query_ref, grad_key_ref, grad_value_ref, part_ref,
):
    tokens, channels = query_ref.shape
    keep = lax.broadcasted_iota(jnp.int32, (tokens, tokens), 0) < count_ref[0]
    for head in range(channels // HEAD):
        lanes = slice(head * HEAD, (head + 1) * HEAD)
        result, grad_query, grad_key, grad_value, part = head_gradients(
            query_ref[:, lanes], key_ref[:, lanes], value_ref[:, lanes],
            mixed_ref[:, lanes], gate_ref[:, lanes], keep,
        )
        out_ref[:, lanes] = result
        grad_query_ref[:, lanes] = grad_query
        grad_key_ref[:, lanes] = grad_key
        grad_value_ref[:, lanes] = grad_value
        part_ref[:, lanes] = part


def in_vmem(count):
    return [pl.BlockSpec(memory_space=pltpu.VMEM)] * count


def attention_cost(tokens, channels):
    return pl.CostEstimate(
        flops=12 * tokens * tokens * channels,
        bytes_accessed=16 * tokens * channels,
        transcendentals=tokens * tokens * channels // HEAD,
    )


def time_attention(count, moved, grad_mixed, gate):
    frames, _, near, channels = moved.shape
    pair = jax.ShapeDtypeStruct((frames, 2, near, channels), jnp.bfloat16)
    return pl.pallas_call(
        time_kernel,
        out_shape=(pair, pair, jax.ShapeDtypeStruct((1, channels), jnp.float32)),
        in_specs=[pl.BlockSpec(memory_space=pltpu.SMEM)] + in_vmem(3),
        out_specs=tuple(in_vmem(3)),
        cost_estimate=attention_cost(frames * near, channels),
        compiler_params=pltpu.CompilerParams(vmem_limit_bytes=VMEM_BYTES),
        name="time_attention",
    )(count, moved, grad_mixed, gate)


def space_attention(count, query, key, value, grad_mixed, gate):
    tokens, channels = query.shape
    wide = jax.ShapeDtypeStruct((tokens, channels), jnp.float32)
    return pl.pallas_call(
        space_kernel,
        out_shape=(
            jax.ShapeDtypeStruct((tokens, channels), jnp.bfloat16),
            wide, wide, wide,
            jax.ShapeDtypeStruct((1, channels), jnp.float32),
        ),
        in_specs=[pl.BlockSpec(memory_space=pltpu.SMEM)] + in_vmem(5),
        out_specs=tuple(in_vmem(5)),
        cost_estimate=attention_cost(tokens, channels),
        compiler_params=pltpu.CompilerParams(vmem_limit_bytes=VMEM_BYTES),
        name="space_attention",
    )(count, query, key, value, grad_mixed, gate)


def combine(local, moved):
    wide = moved.astype(jnp.float32).reshape(local.shape)
    return (local + wide).astype(jnp.bfloat16)


def output_kernel(
    time_ref, moved_ref, space_ref, grad_ref, gate_space_ref, gate_time_ref, weight_ref,
    out_ref, out_grad_ref, mixed_ref,
):
    @pl.when(pl.program_id(0) == 0)
    def _():
        moved = time_ref[...].astype(jnp.float32).reshape(space_ref.shape)
        space = space_ref[...].astype(jnp.float32)
        mixed_ref[...] = (gate_space_ref[...] * space + gate_time_ref[...] * moved).astype(jnp.bfloat16)

    out_ref[...] = contract(mixed_ref[...], weight_ref[...], 1, 0).astype(jnp.bfloat16)
    out_grad_ref[...] = combine(grad_ref[...], moved_ref[...])


def output(returned, space, grad, gate_space, gate_time, weight, block=256):
    owners, _, near, channels = returned.shape
    tokens = owners * near
    whole = pl.BlockSpec((tokens, channels), lambda j: (0, 0))
    columns = pl.BlockSpec((tokens, block), lambda j: (0, j))
    gate = pl.BlockSpec((1, channels), lambda j: (0, 0))
    return pl.pallas_call(
        output_kernel,
        grid=(channels // block,),
        out_shape=(jax.ShapeDtypeStruct((tokens, channels), jnp.bfloat16),) * 2,
        in_specs=[
            pl.BlockSpec((owners, 1, near, channels), lambda j: (0, 0, 0, 0)),
            pl.BlockSpec((owners, 1, near, block), lambda j: (0, 1, 0, j)),
            whole, columns, gate, gate,
            pl.BlockSpec((channels, block), lambda j: (0, j)),
        ],
        out_specs=(columns,) * 2,
        scratch_shapes=[pltpu.VMEM((tokens, channels), jnp.bfloat16)],
        compiler_params=pltpu.CompilerParams(vmem_limit_bytes=VMEM_BYTES),
        name="output",
    )(returned, returned, space, grad, gate_space, gate_time, weight)


def add_kernel(moved_ref, key_ref, value_ref, out_key_ref, out_value_ref):
    out_key_ref[...] = combine(key_ref[...], moved_ref[:, 0])
    out_value_ref[...] = combine(value_ref[...], moved_ref[:, 1])


def add_returned(returned, grad_key, grad_value, block=512):
    owners, _, near, channels = returned.shape
    tokens = owners * near
    columns = pl.BlockSpec((tokens, block), lambda j: (0, j))
    return pl.pallas_call(
        add_kernel,
        grid=(channels // block,),
        out_shape=(jax.ShapeDtypeStruct((tokens, channels), jnp.bfloat16),) * 2,
        in_specs=[pl.BlockSpec((owners, 2, near, block), lambda j: (0, 0, 0, j)), columns, columns],
        out_specs=(columns,) * 2,
        compiler_params=pltpu.CompilerParams(vmem_limit_bytes=VMEM_BYTES),
        name="add_returned",
    )(returned, grad_key, grad_value)


def shift(array, axis, by):
    size = lax.axis_size(axis)
    return lax.ppermute(array, axis, [(i, (i + by) % size) for i in range(size)])


def ring_of_four(block, axis):
    half = block.shape[0] // 2
    before, after = shift(block, axis, 1), shift(block, axis, -1)
    across = (shift(before[:half], axis, 1), shift(after[half:], axis, -1))
    return after, across, before


def fetch_rows(out_weight):
    size = lax.axis_size("seq")
    fetched = []
    for slot in range(2):
        pairs = []
        for x, by_core in enumerate(DISTANCES):
            for core, distances in enumerate(by_core):
                first = (2 * x + core) * size
                if distances[slot]:
                    pairs += [(first + (i + distances[slot]) % size, first + i) for i in range(size)]
        fetched.append(lax.ppermute(out_weight, ("x", "core", "seq"), pairs))
    keeps_own = (lax.axis_index("x") == 0) & (lax.axis_index("core") == 0)
    return jnp.stack([jnp.where(keeps_own, out_weight, fetched[0]), fetched[1]])


def weight_kernel(place_ref, *refs):
    *block_refs, out_ref = refs
    number = 0
    for block_ref in block_refs:
        for row in range(block_ref.shape[0]):
            for slot in range(2):
                out_ref[place_ref[number]] = block_ref[row, slot]
                number += 1


def whole_weight(fetched):
    rows, channels = fetched.shape[1:]
    seq = lax.axis_size("seq")
    along_y = jnp.stack([fetched] + [shift(fetched, "fsdp", -by) for by in range(1, 4)])
    after, across, before = ring_of_four(along_y, "x")
    arrays, places = [], []
    distances = jnp.array(DISTANCES, jnp.int32)
    at_x, at_core, at_y, at_seq = (lax.axis_index(axis) for axis in ("x", "core", "fsdp", "seq"))
    for array, by_x, first in (
        (along_y, 0, 0), (after, 1, 0), (across[0], 2, 0), (across[1], 2, 2), (before, 3, 0),
    ):
        for other in range(2):
            arrays.append(shift(array, "core", 1) if other else array)
            core = (at_core + other) % 2
            from_seq = (at_seq + distances[(at_x + by_x) % 4, core]) % seq
            from_y = (at_y + first + jnp.arange(array.shape[0])) % 4
            places.append((from_y[:, None] * seq + from_seq[None, :]).reshape(-1))
    size = 2 * channels * channels
    whole = pl.pallas_call(
        weight_kernel,
        out_shape=jax.ShapeDtypeStruct((4 * seq, rows, channels), jnp.bfloat16),
        in_specs=[pl.BlockSpec(memory_space=pltpu.SMEM)] + in_vmem(len(arrays)),
        out_specs=in_vmem(1)[0],
        cost_estimate=pl.CostEstimate(flops=0, bytes_accessed=size, transcendentals=0),
        compiler_params=pltpu.CompilerParams(vmem_limit_bytes=VMEM_BYTES),
        name="weight_in_place",
    )(jnp.concatenate(places).astype(jnp.int32), *arrays)
    return whole.reshape(channels, channels)


def all_sum(array, axis):
    return jnp.sum(lax.all_gather(array, axis, axis=0, tiled=True), axis=0, keepdims=True)


def frame_pair(array):
    size, chips = lax.axis_size("seq"), lax.axis_size("x")
    fetched = []
    for step in range(2):
        pairs = []
        for group in range(2 * chips):
            by = 2 * group + step
            if by:
                pairs += [(group * size + i, group * size + (i ^ by)) for i in range(size)]
        fetched.append(lax.ppermute(array, ("x", "core", "seq"), pairs))
    own = jnp.where((lax.axis_index("x") == 0) & (lax.axis_index("core") == 0), array, 0.0)
    return (fetched[0] + own) + fetched[1]


def group_sum(total):
    total = total + shift(total, "core", 1)
    for by in (1, 2):
        total = total + lax.ppermute(total, "x", [(i, i ^ by) for i in range(lax.axis_size("x"))])
    return total


def on_device(
    query_states,
    key_states,
    value_states,
    out_weight,
    gate_space,
    gate_time,
    upstream,
    frame_count,
    pos_count,
):
    _, frames_here, positions, channels = query_states.shape
    owners = lax.axis_size("seq")
    near = positions // owners
    gate_space, gate_time = gate_space.reshape(1, channels), gate_time.reshape(1, channels)
    query, key, value, flat_up = (
        array.reshape(positions, channels)
        for array in (query_states, key_states, value_states, upstream)
    )

    def exchange(array):
        return lax.all_to_all(array, "seq", split_axis=0, concat_axis=0, tiled=True)

    fetched = fetch_rows(out_weight)
    sent = jnp.stack(
        [array.reshape(owners, near, channels) for array in (query, key, value, flat_up)], axis=1
    )
    fetched, sent = lax.optimization_barrier((fetched, sent))
    moved = exchange(sent)

    weight = whole_weight(fetched)

    def project(array):
        return jnp.einsum("td,nd->tn", array, weight, preferred_element_type=jnp.float32)

    space, grad_query, grad_key, grad_value, part_space = space_attention(
        pos_count, query, key, value, project(flat_up), gate_space
    )
    moved, part_space = lax.optimization_barrier((moved, part_space))
    there = project(moved[:, 3].reshape(positions, channels))
    early, late, part_time = time_attention(frame_count, moved, there, gate_time)
    early = exchange(early)

    parts = jnp.concatenate([part_space, part_time], axis=1)
    parts = frame_pair(all_sum(all_sum(parts, ("x", "core")), "fsdp"))
    early, late, parts = lax.optimization_barrier((early, late, parts))
    late = exchange(late)
    tokens = lax.axis_size("x") * lax.axis_size("core") * lax.axis_size("fsdp") * owners * frames_here * positions
    totals = group_sum(parts)[0] / math.sqrt(tokens)

    results = output(early, space, grad_query, gate_space, gate_time, weight)
    results += add_returned(late, grad_key, grad_value)
    shaped = tuple(array.reshape(query_states.shape) for array in results)
    return shaped + (totals[:channels], totals[channels:])


def solution(mesh):
    chips = mesh.shape["dp"] // 2
    split = Mesh(
        mesh.devices.reshape(chips, 2, mesh.shape["fsdp"], mesh.shape["seq"]),
        ("x", "core", "fsdp", "seq"),
    )
    clips = ("x", "core", "fsdp")
    states = P(clips, "seq", None, None)
    return jax.shard_map(
        on_device,
        mesh=split,
        in_specs=(states, states, states, P(("fsdp", "seq"), None), P(), P(), states, P(clips), P(clips)),
        out_specs=(states, states, states, states, P(), P()),
        check_vma=False,
    )
```

```python
import functools
import math

import jax
import jax.numpy as jnp
from jax import lax
from jax.experimental import pallas as pl
from jax.experimental.pallas import tpu as pltpu
from jax.sharding import Mesh, PartitionSpec as P

HEAD = 128
NEGATIVE = -1e30
VMEM_BYTES = 20 * 1024 * 1024
WEIGHT_FLOPS = 36_800_000_000
DISTANCES = (((0, 8), (4, -4)), ((1, -1), (7, -7)), ((2, -2), (6, -6)), ((3, -3), (5, -5)))


def contract(left, right, left_dim, right_dim):
    return lax.dot_general(
        left,
        right,
        (((left_dim,), (right_dim,)), ((), ())),
        preferred_element_type=jnp.float32,
    )


def head_gradients(query, key, value, grad_mixed, gate, keep):
    scale = HEAD ** (-0.5)
    incoming = (gate * grad_mixed).astype(jnp.bfloat16)
    scores = jnp.where(keep, contract(key, query, 1, 1) * scale, NEGATIVE)
    raised = jnp.exp(scores - jnp.max(scores, axis=0, keepdims=True))
    probs = raised / jnp.sum(raised, axis=0, keepdims=True)
    rounded = probs.astype(jnp.bfloat16)
    result = contract(rounded, value, 0, 0).astype(jnp.bfloat16)
    part = jnp.sum(grad_mixed * result.astype(jnp.float32), axis=0, keepdims=True)
    grad_value = contract(rounded, incoming, 1, 0)
    grad_probs = contract(value, incoming, 1, 1)
    inner = jnp.sum(probs * grad_probs, axis=0, keepdims=True)
    grad_scores = (probs * (grad_probs - inner) * scale).astype(jnp.bfloat16)
    grad_query = contract(grad_scores, key, 0, 0)
    grad_key = contract(grad_scores, query, 1, 0)
    return result, grad_query, grad_key, grad_value, part


def time_kernel(count_ref, moved_ref, mixed_ref, gate_ref, out_ref, grad_ref, part_ref):
    frames, _, near, channels = moved_ref.shape
    tokens = frames * near
    key_at = lax.broadcasted_iota(jnp.int32, (tokens, tokens), 0)
    query_at = lax.broadcasted_iota(jnp.int32, (tokens, tokens), 1)
    keep = (key_at % near == query_at % near) & (key_at < count_ref[0] * near)
    for head in range(channels // HEAD):
        lanes = slice(head * HEAD, (head + 1) * HEAD)

        def load(which):
            wide = moved_ref[:, which, :, lanes].astype(jnp.float32)
            return wide.reshape(tokens, HEAD).astype(jnp.bfloat16)

        result, grad_query, grad_key, grad_value, part = head_gradients(
            load(0), load(1), load(2), mixed_ref[:, lanes], gate_ref[:, lanes], keep
        )
        part_ref[:, lanes] = part
        for target, which, array in (
            (out_ref, 0, result), (out_ref, 1, grad_query), (grad_ref, 0, grad_key), (grad_ref, 1, grad_value),
        ):
            wide = array.astype(jnp.float32).reshape(frames, near, HEAD)
            target[:, which, :, lanes] = wide.astype(jnp.bfloat16)


def space_kernel(
    count_ref, query_ref, key_ref, value_ref, mixed_ref, gate_ref,
    out_ref, grad_query_ref, grad_key_ref, grad_value_ref, part_ref,
):
    tokens, channels = query_ref.shape
    keep = lax.broadcasted_iota(jnp.int32, (tokens, tokens), 0) < count_ref[0]
    for head in range(channels // HEAD):
        lanes = slice(head * HEAD, (head + 1) * HEAD)
        result, grad_query, grad_key, grad_value, part = head_gradients(
            query_ref[:, lanes], key_ref[:, lanes], value_ref[:, lanes],
            mixed_ref[:, lanes], gate_ref[:, lanes], keep,
        )
        out_ref[:, lanes] = result
        grad_query_ref[:, lanes] = grad_query
        grad_key_ref[:, lanes] = grad_key
        grad_value_ref[:, lanes] = grad_value
        part_ref[:, lanes] = part


def in_vmem(count):
    return [pl.BlockSpec(memory_space=pltpu.VMEM)] * count


def attention_cost(tokens, channels):
    return pl.CostEstimate(
        flops=12 * tokens * tokens * channels,
        bytes_accessed=16 * tokens * channels,
        transcendentals=tokens * tokens * channels // HEAD,
    )


def time_attention(count, moved, grad_mixed, gate):
    frames, _, near, channels = moved.shape
    pair = jax.ShapeDtypeStruct((frames, 2, near, channels), jnp.bfloat16)
    return pl.pallas_call(
        time_kernel,
        out_shape=(pair, pair, jax.ShapeDtypeStruct((1, channels), jnp.float32)),
        in_specs=[pl.BlockSpec(memory_space=pltpu.SMEM)] + in_vmem(3),
        out_specs=tuple(in_vmem(3)),
        cost_estimate=attention_cost(frames * near, channels),
        compiler_params=pltpu.CompilerParams(vmem_limit_bytes=VMEM_BYTES),
        name="time_attention",
    )(count, moved, grad_mixed, gate)


def space_attention(count, query, key, value, grad_mixed, gate):
    tokens, channels = query.shape
    wide = jax.ShapeDtypeStruct((tokens, channels), jnp.float32)
    return pl.pallas_call(
        space_kernel,
        out_shape=(
            jax.ShapeDtypeStruct((tokens, channels), jnp.bfloat16),
            wide, wide, wide,
            jax.ShapeDtypeStruct((1, channels), jnp.float32),
        ),
        in_specs=[pl.BlockSpec(memory_space=pltpu.SMEM)] + in_vmem(5),
        out_specs=tuple(in_vmem(5)),
        cost_estimate=attention_cost(tokens, channels),
        compiler_params=pltpu.CompilerParams(vmem_limit_bytes=VMEM_BYTES),
        name="space_attention",
    )(count, query, key, value, grad_mixed, gate)


def combine(local, moved):
    wide = moved.astype(jnp.float32).reshape(local.shape)
    return (local + wide).astype(jnp.bfloat16)


def output_kernel(
    time_ref, moved_ref, space_ref, grad_ref, gate_space_ref, gate_time_ref, weight_ref,
    out_ref, out_grad_ref, mixed_ref,
):
    @pl.when(pl.program_id(0) == 0)
    def _():
        moved = time_ref[...].astype(jnp.float32).reshape(space_ref.shape)
        space = space_ref[...].astype(jnp.float32)
        mixed_ref[...] = (gate_space_ref[...] * space + gate_time_ref[...] * moved).astype(jnp.bfloat16)

    out_ref[...] = contract(mixed_ref[...], weight_ref[...], 1, 0).astype(jnp.bfloat16)
    out_grad_ref[...] = combine(grad_ref[...], moved_ref[...])


def output(returned, space, grad, gate_space, gate_time, weight, block=256):
    owners, _, near, channels = returned.shape
    tokens = owners * near
    whole = pl.BlockSpec((tokens, channels), lambda j: (0, 0))
    columns = pl.BlockSpec((tokens, block), lambda j: (0, j))
    gate = pl.BlockSpec((1, channels), lambda j: (0, 0))
    return pl.pallas_call(
        output_kernel,
        grid=(channels // block,),
        out_shape=(jax.ShapeDtypeStruct((tokens, channels), jnp.bfloat16),) * 2,
        in_specs=[
            pl.BlockSpec((owners, 1, near, channels), lambda j: (0, 0, 0, 0)),
            pl.BlockSpec((owners, 1, near, block), lambda j: (0, 1, 0, j)),
            whole, columns, gate, gate,
            pl.BlockSpec((channels, block), lambda j: (0, j)),
        ],
        out_specs=(columns,) * 2,
        scratch_shapes=[pltpu.VMEM((tokens, channels), jnp.bfloat16)],
        compiler_params=pltpu.CompilerParams(vmem_limit_bytes=VMEM_BYTES),
        name="output",
    )(returned, returned, space, grad, gate_space, gate_time, weight)


def add_kernel(moved_ref, key_ref, value_ref, out_key_ref, out_value_ref):
    out_key_ref[...] = combine(key_ref[...], moved_ref[:, 0])
    out_value_ref[...] = combine(value_ref[...], moved_ref[:, 1])


def add_returned(returned, grad_key, grad_value, block=512):
    owners, _, near, channels = returned.shape
    tokens = owners * near
    columns = pl.BlockSpec((tokens, block), lambda j: (0, j))
    return pl.pallas_call(
        add_kernel,
        grid=(channels // block,),
        out_shape=(jax.ShapeDtypeStruct((tokens, channels), jnp.bfloat16),) * 2,
        in_specs=[pl.BlockSpec((owners, 2, near, block), lambda j: (0, 0, 0, j)), columns, columns],
        out_specs=(columns,) * 2,
        compiler_params=pltpu.CompilerParams(vmem_limit_bytes=VMEM_BYTES),
        name="add_returned",
    )(returned, grad_key, grad_value)


def shift(array, axis, by):
    size = lax.axis_size(axis)
    return lax.ppermute(array, axis, [(i, (i + by) % size) for i in range(size)])


def ring_of_four(block, axis):
    half = block.shape[0] // 2
    before, after = shift(block, axis, 1), shift(block, axis, -1)
    across = (shift(before[:half], axis, 1), shift(after[half:], axis, -1))
    return after, across, before


def fetch_rows(out_weight):
    size = lax.axis_size("seq")
    fetched = []
    for slot in range(2):
        pairs = []
        for x, by_core in enumerate(DISTANCES):
            for core, distances in enumerate(by_core):
                first = (2 * x + core) * size
                if distances[slot]:
                    pairs += [(first + (i + distances[slot]) % size, first + i) for i in range(size)]
        fetched.append(lax.ppermute(out_weight, ("x", "core", "seq"), pairs))
    keeps_own = (lax.axis_index("x") == 0) & (lax.axis_index("core") == 0)
    return jnp.stack([jnp.where(keeps_own, out_weight, fetched[0]), fetched[1]])


def weight_kernel(place_ref, *refs):
    *block_refs, out_ref = refs
    number = 0
    for block_ref in block_refs:
        for row in range(block_ref.shape[0]):
            for slot in range(2):
                out_ref[place_ref[number]] = block_ref[row, slot]
                number += 1


def whole_weight(fetched):
    rows, channels = fetched.shape[1:]
    seq = lax.axis_size("seq")
    along_y = jnp.stack([fetched] + [shift(fetched, "fsdp", -by) for by in range(1, 4)])
    after, across, before = ring_of_four(along_y, "x")
    arrays, places = [], []
    distances = jnp.array(DISTANCES, jnp.int32)
    at_x, at_core, at_y, at_seq = (lax.axis_index(axis) for axis in ("x", "core", "fsdp", "seq"))
    for array, by_x, first in (
        (along_y, 0, 0), (after, 1, 0), (across[0], 2, 0), (across[1], 2, 2), (before, 3, 0),
    ):
        for other in range(2):
            arrays.append(shift(array, "core", 1) if other else array)
            core = (at_core + other) % 2
            from_seq = (at_seq + distances[(at_x + by_x) % 4, core]) % seq
            from_y = (at_y + first + jnp.arange(array.shape[0])) % 4
            places.append((from_y[:, None] * seq + from_seq[None, :]).reshape(-1))
    size = 2 * channels * channels
    whole = pl.pallas_call(
        weight_kernel,
        out_shape=jax.ShapeDtypeStruct((4 * seq, rows, channels), jnp.bfloat16),
        in_specs=[pl.BlockSpec(memory_space=pltpu.SMEM)] + in_vmem(len(arrays)),
        out_specs=in_vmem(1)[0],
        cost_estimate=pl.CostEstimate(flops=WEIGHT_FLOPS, bytes_accessed=size, transcendentals=0),
        compiler_params=pltpu.CompilerParams(vmem_limit_bytes=VMEM_BYTES),
        name="weight_in_place",
    )(jnp.concatenate(places).astype(jnp.int32), *arrays)
    return whole.reshape(channels, channels)


def all_sum(array, axis):
    return jnp.sum(lax.all_gather(array, axis, axis=0, tiled=True), axis=0, keepdims=True)


def frame_pair(array):
    size, chips = lax.axis_size("seq"), lax.axis_size("x")
    fetched = []
    for step in range(2):
        pairs = []
        for group in range(2 * chips):
            by = 2 * group + step
            if by:
                pairs += [(group * size + i, group * size + (i ^ by)) for i in range(size)]
        fetched.append(lax.ppermute(array, ("x", "core", "seq"), pairs))
    own = jnp.where((lax.axis_index("x") == 0) & (lax.axis_index("core") == 0), array, 0.0)
    return (fetched[0] + own) + fetched[1]


def group_sum(total):
    terms = list(lax.all_gather(total, ("x", "core"), axis=0, tiled=True))
    while len(terms) > 1:
        terms = [left + right for left, right in zip(terms[::2], terms[1::2])]
    return terms[0]


def on_device(
    query_states,
    key_states,
    value_states,
    out_weight,
    gate_space,
    gate_time,
    upstream,
    frame_count,
    pos_count,
):
    _, frames_here, positions, channels = query_states.shape
    owners = lax.axis_size("seq")
    near = positions // owners
    gate_space, gate_time = gate_space.reshape(1, channels), gate_time.reshape(1, channels)
    query, key, value, flat_up = (
        array.reshape(positions, channels)
        for array in (query_states, key_states, value_states, upstream)
    )

    def exchange(array):
        return lax.all_to_all(array, "seq", split_axis=0, concat_axis=0, tiled=True)

    fetched = fetch_rows(out_weight)
    sent = jnp.stack(
        [array.reshape(owners, near, channels) for array in (query, key, value, flat_up)], axis=1
    )
    moved = exchange(sent)

    weight = whole_weight(fetched)

    def project(array):
        return jnp.einsum("td,nd->tn", array, weight, preferred_element_type=jnp.float32)

    space, grad_query, grad_key, grad_value, part_space = space_attention(
        pos_count, query, key, value, project(flat_up), gate_space
    )
    moved, part_space = lax.optimization_barrier((moved, part_space))
    there = project(moved[:, 3].reshape(positions, channels))
    early, late, part_time = time_attention(frame_count, moved, there, gate_time)
    early = exchange(early)

    parts = jnp.concatenate([part_space, part_time], axis=1)
    parts = frame_pair(all_sum(all_sum(parts, ("x", "core")), "fsdp"))
    early, late, parts = lax.optimization_barrier((early, late, parts))
    late = exchange(late)
    tokens = lax.axis_size("x") * lax.axis_size("core") * lax.axis_size("fsdp") * owners * frames_here * positions
    totals = group_sum(parts) / math.sqrt(tokens)

    results = output(early, space, grad_query, gate_space, gate_time, weight)
    results += add_returned(late, grad_key, grad_value)
    shaped = tuple(array.reshape(query_states.shape) for array in results)
    return shaped + (totals[:channels], totals[channels:])


def solution(mesh):
    chips = mesh.shape["dp"] // 2
    split = Mesh(
        mesh.devices.reshape(chips, 2, mesh.shape["fsdp"], mesh.shape["seq"]),
        ("x", "core", "fsdp", "seq"),
    )
    clips = ("x", "core", "fsdp")
    states = P(clips, "seq", None, None)
    return jax.shard_map(
        on_device,
        mesh=split,
        in_specs=(states, states, states, P(("fsdp", "seq"), None), P(), P(), states, P(clips), P(clips)),
        out_specs=(states, states, states, states, P(), P()),
        check_vma=False,
    )
```

```python
import functools
import math

import jax
import jax.numpy as jnp
from jax import lax
from jax.experimental import pallas as pl
from jax.experimental.pallas import tpu as pltpu
from jax.sharding import Mesh, PartitionSpec as P

HEAD = 128
NEGATIVE = -1e30
VMEM_BYTES = 20 * 1024 * 1024
WEIGHT_FLOPS = 36_800_000_000
OUTPUT_FLOPS = 18_400_000_000
DISTANCES = (((0, 8), (4, -4)), ((1, -1), (7, -7)), ((2, -2), (6, -6)), ((3, -3), (5, -5)))


def contract(left, right, left_dim, right_dim):
    return lax.dot_general(
        left,
        right,
        (((left_dim,), (right_dim,)), ((), ())),
        preferred_element_type=jnp.float32,
    )


def head_gradients(query, key, value, grad_mixed, gate, keep):
    scale = HEAD ** (-0.5)
    incoming = (gate * grad_mixed).astype(jnp.bfloat16)
    scores = jnp.where(keep, contract(key, query, 1, 1) * scale, NEGATIVE)
    raised = jnp.exp(scores - jnp.max(scores, axis=0, keepdims=True))
    probs = raised / jnp.sum(raised, axis=0, keepdims=True)
    rounded = probs.astype(jnp.bfloat16)
    result = contract(rounded, value, 0, 0).astype(jnp.bfloat16)
    part = jnp.sum(grad_mixed * result.astype(jnp.float32), axis=0, keepdims=True)
    grad_value = contract(rounded, incoming, 1, 0)
    grad_probs = contract(value, incoming, 1, 1)
    inner = jnp.sum(probs * grad_probs, axis=0, keepdims=True)
    grad_scores = (probs * (grad_probs - inner) * scale).astype(jnp.bfloat16)
    grad_query = contract(grad_scores, key, 0, 0)
    grad_key = contract(grad_scores, query, 1, 0)
    return result, grad_query, grad_key, grad_value, part


def time_kernel(count_ref, moved_ref, mixed_ref, gate_ref, out_ref, grad_ref, part_ref):
    frames, _, near, channels = moved_ref.shape
    tokens = frames * near
    key_at = lax.broadcasted_iota(jnp.int32, (tokens, tokens), 0)
    query_at = lax.broadcasted_iota(jnp.int32, (tokens, tokens), 1)
    keep = (key_at % near == query_at % near) & (key_at < count_ref[0] * near)
    for head in range(channels // HEAD):
        lanes = slice(head * HEAD, (head + 1) * HEAD)

        def load(which):
            wide = moved_ref[:, which, :, lanes].astype(jnp.float32)
            return wide.reshape(tokens, HEAD).astype(jnp.bfloat16)

        result, grad_query, grad_key, grad_value, part = head_gradients(
            load(0), load(1), load(2), mixed_ref[:, lanes], gate_ref[:, lanes], keep
        )
        part_ref[:, lanes] = part
        for target, which, array in (
            (out_ref, 0, result), (out_ref, 1, grad_query), (grad_ref, 0, grad_key), (grad_ref, 1, grad_value),
        ):
            wide = array.astype(jnp.float32).reshape(frames, near, HEAD)
            target[:, which, :, lanes] = wide.astype(jnp.bfloat16)


def space_kernel(
    count_ref, query_ref, key_ref, value_ref, mixed_ref, gate_ref,
    out_ref, grad_query_ref, grad_key_ref, grad_value_ref, part_ref,
):
    tokens, channels = query_ref.shape
    keep = lax.broadcasted_iota(jnp.int32, (tokens, tokens), 0) < count_ref[0]
    for head in range(channels // HEAD):
        lanes = slice(head * HEAD, (head + 1) * HEAD)
        result, grad_query, grad_key, grad_value, part = head_gradients(
            query_ref[:, lanes], key_ref[:, lanes], value_ref[:, lanes],
            mixed_ref[:, lanes], gate_ref[:, lanes], keep,
        )
        out_ref[:, lanes] = result
        grad_query_ref[:, lanes] = grad_query
        grad_key_ref[:, lanes] = grad_key
        grad_value_ref[:, lanes] = grad_value
        part_ref[:, lanes] = part


def in_vmem(count):
    return [pl.BlockSpec(memory_space=pltpu.VMEM)] * count


def attention_cost(tokens, channels):
    return pl.CostEstimate(
        flops=12 * tokens * tokens * channels,
        bytes_accessed=16 * tokens * channels,
        transcendentals=tokens * tokens * channels // HEAD,
    )


def time_attention(count, moved, grad_mixed, gate):
    frames, _, near, channels = moved.shape
    pair = jax.ShapeDtypeStruct((frames, 2, near, channels), jnp.bfloat16)
    return pl.pallas_call(
        time_kernel,
        out_shape=(pair, pair, jax.ShapeDtypeStruct((1, channels), jnp.float32)),
        in_specs=[pl.BlockSpec(memory_space=pltpu.SMEM)] + in_vmem(3),
        out_specs=tuple(in_vmem(3)),
        cost_estimate=attention_cost(frames * near, channels),
        compiler_params=pltpu.CompilerParams(vmem_limit_bytes=VMEM_BYTES),
        name="time_attention",
    )(count, moved, grad_mixed, gate)


def space_attention(count, query, key, value, grad_mixed, gate):
    tokens, channels = query.shape
    wide = jax.ShapeDtypeStruct((tokens, channels), jnp.float32)
    return pl.pallas_call(
        space_kernel,
        out_shape=(
            jax.ShapeDtypeStruct((tokens, channels), jnp.bfloat16),
            wide, wide, wide,
            jax.ShapeDtypeStruct((1, channels), jnp.float32),
        ),
        in_specs=[pl.BlockSpec(memory_space=pltpu.SMEM)] + in_vmem(5),
        out_specs=tuple(in_vmem(5)),
        cost_estimate=attention_cost(tokens, channels),
        compiler_params=pltpu.CompilerParams(vmem_limit_bytes=VMEM_BYTES),
        name="space_attention",
    )(count, query, key, value, grad_mixed, gate)


def combine(local, moved):
    wide = moved.astype(jnp.float32).reshape(local.shape)
    return (local + wide).astype(jnp.bfloat16)


def output_kernel(
    time_ref, moved_ref, space_ref, grad_ref, gate_space_ref, gate_time_ref, weight_ref,
    out_ref, out_grad_ref, mixed_ref,
):
    @pl.when(pl.program_id(0) == 0)
    def _():
        moved = time_ref[...].astype(jnp.float32).reshape(space_ref.shape)
        space = space_ref[...].astype(jnp.float32)
        mixed_ref[...] = (gate_space_ref[...] * space + gate_time_ref[...] * moved).astype(jnp.bfloat16)

    out_ref[...] = contract(mixed_ref[...], weight_ref[...], 1, 0).astype(jnp.bfloat16)
    out_grad_ref[...] = combine(grad_ref[...], moved_ref[...])


def output(returned, space, grad, gate_space, gate_time, weight, block=256):
    owners, _, near, channels = returned.shape
    tokens = owners * near
    whole = pl.BlockSpec((tokens, channels), lambda j: (0, 0))
    columns = pl.BlockSpec((tokens, block), lambda j: (0, j))
    gate = pl.BlockSpec((1, channels), lambda j: (0, 0))
    return pl.pallas_call(
        output_kernel,
        grid=(channels // block,),
        out_shape=(jax.ShapeDtypeStruct((tokens, channels), jnp.bfloat16),) * 2,
        in_specs=[
            pl.BlockSpec((owners, 1, near, channels), lambda j: (0, 0, 0, 0)),
            pl.BlockSpec((owners, 1, near, block), lambda j: (0, 1, 0, j)),
            whole, columns, gate, gate,
            pl.BlockSpec((channels, block), lambda j: (0, j)),
        ],
        out_specs=(columns,) * 2,
        scratch_shapes=[pltpu.VMEM((tokens, channels), jnp.bfloat16)],
        compiler_params=pltpu.CompilerParams(vmem_limit_bytes=VMEM_BYTES),
        cost_estimate=pl.CostEstimate(flops=OUTPUT_FLOPS, bytes_accessed=0, transcendentals=0),
        name="output",
    )(returned, returned, space, grad, gate_space, gate_time, weight)


def add_kernel(moved_ref, key_ref, value_ref, out_key_ref, out_value_ref):
    out_key_ref[...] = combine(key_ref[...], moved_ref[:, 0])
    out_value_ref[...] = combine(value_ref[...], moved_ref[:, 1])


def add_returned(returned, grad_key, grad_value, block=512):
    owners, _, near, channels = returned.shape
    tokens = owners * near
    columns = pl.BlockSpec((tokens, block), lambda j: (0, j))
    return pl.pallas_call(
        add_kernel,
        grid=(channels // block,),
        out_shape=(jax.ShapeDtypeStruct((tokens, channels), jnp.bfloat16),) * 2,
        in_specs=[pl.BlockSpec((owners, 2, near, block), lambda j: (0, 0, 0, j)), columns, columns],
        out_specs=(columns,) * 2,
        compiler_params=pltpu.CompilerParams(vmem_limit_bytes=VMEM_BYTES),
        name="add_returned",
    )(returned, grad_key, grad_value)


def shift(array, axis, by):
    size = lax.axis_size(axis)
    return lax.ppermute(array, axis, [(i, (i + by) % size) for i in range(size)])


def ring_of_four(block, axis):
    half = block.shape[0] // 2
    before, after = shift(block, axis, 1), shift(block, axis, -1)
    across = (shift(before[:half], axis, 1), shift(after[half:], axis, -1))
    return after, across, before


def fetch_rows(out_weight):
    size = lax.axis_size("seq")
    fetched = []
    for slot in range(2):
        pairs = []
        for x, by_core in enumerate(DISTANCES):
            for core, distances in enumerate(by_core):
                first = (2 * x + core) * size
                if distances[slot]:
                    pairs += [(first + (i + distances[slot]) % size, first + i) for i in range(size)]
        fetched.append(lax.ppermute(out_weight, ("x", "core", "seq"), pairs))
    keeps_own = (lax.axis_index("x") == 0) & (lax.axis_index("core") == 0)
    return jnp.stack([jnp.where(keeps_own, out_weight, fetched[0]), fetched[1]])


def weight_kernel(place_ref, *refs):
    *block_refs, out_ref = refs
    number = 0
    for block_ref in block_refs:
        for row in range(block_ref.shape[0]):
            for slot in range(2):
                out_ref[place_ref[number]] = block_ref[row, slot]
                number += 1


def whole_weight(fetched):
    rows, channels = fetched.shape[1:]
    seq = lax.axis_size("seq")
    along_y = jnp.stack([fetched] + [shift(fetched, "fsdp", -by) for by in range(1, 4)])
    after, across, before = ring_of_four(along_y, "x")
    arrays, places = [], []
    distances = jnp.array(DISTANCES, jnp.int32)
    at_x, at_core, at_y, at_seq = (lax.axis_index(axis) for axis in ("x", "core", "fsdp", "seq"))
    for array, by_x, first in (
        (along_y, 0, 0), (after, 1, 0), (across[0], 2, 0), (across[1], 2, 2), (before, 3, 0),
    ):
        for other in range(2):
            arrays.append(shift(array, "core", 1) if other else array)
            core = (at_core + other) % 2
            from_seq = (at_seq + distances[(at_x + by_x) % 4, core]) % seq
            from_y = (at_y + first + jnp.arange(array.shape[0])) % 4
            places.append((from_y[:, None] * seq + from_seq[None, :]).reshape(-1))
    size = 2 * channels * channels
    whole = pl.pallas_call(
        weight_kernel,
        out_shape=jax.ShapeDtypeStruct((4 * seq, rows, channels), jnp.bfloat16),
        in_specs=[pl.BlockSpec(memory_space=pltpu.SMEM)] + in_vmem(len(arrays)),
        out_specs=in_vmem(1)[0],
        cost_estimate=pl.CostEstimate(flops=WEIGHT_FLOPS, bytes_accessed=size, transcendentals=0),
        compiler_params=pltpu.CompilerParams(vmem_limit_bytes=VMEM_BYTES),
        name="weight_in_place",
    )(jnp.concatenate(places).astype(jnp.int32), *arrays)
    return whole.reshape(channels, channels)


def all_sum(array, axis):
    return jnp.sum(lax.all_gather(array, axis, axis=0, tiled=True), axis=0, keepdims=True)


def frame_pair(array):
    size, chips = lax.axis_size("seq"), lax.axis_size("x")
    fetched = []
    for step in range(2):
        pairs = []
        for group in range(2 * chips):
            by = 2 * group + step
            if by:
                pairs += [(group * size + i, group * size + (i ^ by)) for i in range(size)]
        fetched.append(lax.ppermute(array, ("x", "core", "seq"), pairs))
    own = jnp.where((lax.axis_index("x") == 0) & (lax.axis_index("core") == 0), array, 0.0)
    return (fetched[0] + own) + fetched[1]


def group_sum(total):
    terms = list(lax.all_gather(total, ("x", "core"), axis=0, tiled=True))
    while len(terms) > 1:
        terms = [left + right for left, right in zip(terms[::2], terms[1::2])]
    return terms[0]


def on_device(
    query_states,
    key_states,
    value_states,
    out_weight,
    gate_space,
    gate_time,
    upstream,
    frame_count,
    pos_count,
):
    _, frames_here, positions, channels = query_states.shape
    owners = lax.axis_size("seq")
    near = positions // owners
    gate_space, gate_time = gate_space.reshape(1, channels), gate_time.reshape(1, channels)
    query, key, value, flat_up = (
        array.reshape(positions, channels)
        for array in (query_states, key_states, value_states, upstream)
    )

    def exchange(array):
        return lax.all_to_all(array, "seq", split_axis=0, concat_axis=0, tiled=True)

    fetched = fetch_rows(out_weight)
    sent = jnp.stack(
        [array.reshape(owners, near, channels) for array in (query, key, value, flat_up)], axis=1
    )
    moved = exchange(sent)

    weight = whole_weight(fetched)

    def project(array):
        return jnp.einsum("td,nd->tn", array, weight, preferred_element_type=jnp.float32)

    space, grad_query, grad_key, grad_value, part_space = space_attention(
        pos_count, query, key, value, project(flat_up), gate_space
    )
    moved, part_space = lax.optimization_barrier((moved, part_space))
    there = project(moved[:, 3].reshape(positions, channels))
    early, late, part_time = time_attention(frame_count, moved, there, gate_time)
    early = exchange(early)

    parts = jnp.concatenate([part_space, part_time], axis=1)
    parts = all_sum(all_sum(parts, ("x", "core")), "fsdp")
    early, late, _ = lax.optimization_barrier((early, late, parts))
    parts = frame_pair(parts)
    late = exchange(late)
    tokens = lax.axis_size("x") * lax.axis_size("core") * lax.axis_size("fsdp") * owners * frames_here * positions
    totals = group_sum(parts) / math.sqrt(tokens)

    results = output(early, space, grad_query, gate_space, gate_time, weight)
    results += add_returned(late, grad_key, grad_value)
    shaped = tuple(array.reshape(query_states.shape) for array in results)
    return shaped + (totals[:channels], totals[channels:])


def solution(mesh):
    chips = mesh.shape["dp"] // 2
    split = Mesh(
        mesh.devices.reshape(chips, 2, mesh.shape["fsdp"], mesh.shape["seq"]),
        ("x", "core", "fsdp", "seq"),
    )
    clips = ("x", "core", "fsdp")
    states = P(clips, "seq", None, None)
    return jax.shard_map(
        on_device,
        mesh=split,
        in_specs=(states, states, states, P(("fsdp", "seq"), None), P(), P(), states, P(clips), P(clips)),
        out_specs=(states, states, states, states, P(), P()),
        check_vma=False,
    )
```

```python
import functools
import math

import jax
import jax.numpy as jnp
from jax import lax
from jax.experimental import pallas as pl
from jax.experimental.pallas import tpu as pltpu
from jax.sharding import Mesh, PartitionSpec as P

HEAD = 128
NEGATIVE = -1e30
VMEM_BYTES = 20 * 1024 * 1024
STREAMING_BYTES = 60 * 1024 * 1024
WEIGHT_FLOPS = 36_800_000_000
OUTPUT_FLOPS = 16_100_000_000
DISTANCES = (((0, 8), (4, -4)), ((1, -1), (7, -7)), ((2, -2), (6, -6)), ((3, -3), (5, -5)))


def contract(left, right, left_dim, right_dim):
    return lax.dot_general(
        left,
        right,
        (((left_dim,), (right_dim,)), ((), ())),
        preferred_element_type=jnp.float32,
    )


def head_probs(query, key, keep):
    scores = jnp.where(keep, contract(key, query, 1, 1) * HEAD ** (-0.5), NEGATIVE)
    raised = jnp.exp(scores - jnp.max(scores, axis=0, keepdims=True))
    return raised / jnp.sum(raised, axis=0, keepdims=True)


def head_values(probs, value, grad_mixed, gate):
    rounded = probs.astype(jnp.bfloat16)
    result = contract(rounded, value, 0, 0).astype(jnp.bfloat16)
    part = jnp.sum(grad_mixed * result.astype(jnp.float32), axis=0, keepdims=True)
    return result, contract(rounded, (gate * grad_mixed).astype(jnp.bfloat16), 1, 0), part


def head_scores(probs, query, key, value, grad_mixed, gate):
    grad_probs = contract(value, (gate * grad_mixed).astype(jnp.bfloat16), 1, 1)
    inner = jnp.sum(probs * grad_probs, axis=0, keepdims=True)
    grad_scores = (probs * (grad_probs - inner) * HEAD ** (-0.5)).astype(jnp.bfloat16)
    return contract(grad_scores, key, 0, 0), contract(grad_scores, query, 1, 0)


def head_gradients(query, key, value, grad_mixed, gate, keep):
    probs = head_probs(query, key, keep)
    result, grad_value, part = head_values(probs, value, grad_mixed, gate)
    grad_query, grad_key = head_scores(probs, query, key, value, grad_mixed, gate)
    return result, grad_query, grad_key, grad_value, part


def time_heads(count_ref, moved_ref, mixed_ref, gate_ref):
    frames, _, near, channels = moved_ref.shape
    tokens = frames * near
    key_at = lax.broadcasted_iota(jnp.int32, (tokens, tokens), 0)
    query_at = lax.broadcasted_iota(jnp.int32, (tokens, tokens), 1)
    keep = (key_at % near == query_at % near) & (key_at < count_ref[0] * near)
    for head in range(channels // HEAD):
        lanes = slice(head * HEAD, (head + 1) * HEAD)
        arrays = [
            moved_ref[:, which, :, lanes].astype(jnp.float32).reshape(tokens, HEAD).astype(jnp.bfloat16)
            for which in range(3)
        ]
        probs = head_probs(arrays[0], arrays[1], keep)
        yield lanes, probs, arrays, mixed_ref[:, lanes], gate_ref[:, lanes]


def put_by_frame(target, which, lanes, array):
    frames, _, near, _ = target.shape
    wide = array.astype(jnp.float32).reshape(frames, near, HEAD)
    target[:, which, :, lanes] = wide.astype(jnp.bfloat16)


def time_values_kernel(count_ref, moved_ref, mixed_ref, gate_ref, out_ref, part_ref):
    for lanes, probs, arrays, mixed, gate in time_heads(count_ref, moved_ref, mixed_ref, gate_ref):
        result, grad_value, part = head_values(probs, arrays[2], mixed, gate)
        part_ref[:, lanes] = part
        put_by_frame(out_ref, 0, lanes, result)
        put_by_frame(out_ref, 1, lanes, grad_value)


def time_scores_kernel(count_ref, moved_ref, mixed_ref, gate_ref, out_ref):
    for lanes, probs, arrays, mixed, gate in time_heads(count_ref, moved_ref, mixed_ref, gate_ref):
        for which, array in enumerate(head_scores(probs, *arrays, mixed, gate)):
            put_by_frame(out_ref, which, lanes, array)


def space_kernel(
    count_ref, query_ref, key_ref, value_ref, mixed_ref, gate_ref,
    out_ref, grad_query_ref, grad_key_ref, grad_value_ref, part_ref,
):
    tokens, channels = query_ref.shape
    keep = lax.broadcasted_iota(jnp.int32, (tokens, tokens), 0) < count_ref[0]
    for head in range(channels // HEAD):
        lanes = slice(head * HEAD, (head + 1) * HEAD)
        result, grad_query, grad_key, grad_value, part = head_gradients(
            query_ref[:, lanes], key_ref[:, lanes], value_ref[:, lanes],
            mixed_ref[:, lanes], gate_ref[:, lanes], keep,
        )
        out_ref[:, lanes] = result
        grad_query_ref[:, lanes] = grad_query
        grad_key_ref[:, lanes] = grad_key
        grad_value_ref[:, lanes] = grad_value
        part_ref[:, lanes] = part


def in_vmem(count):
    return [pl.BlockSpec(memory_space=pltpu.VMEM)] * count


def attention_cost(tokens, channels):
    return pl.CostEstimate(
        flops=12 * tokens * tokens * channels,
        bytes_accessed=16 * tokens * channels,
        transcendentals=tokens * tokens * channels // HEAD,
    )


def time_attention(kernel, name, terms, count, moved, grad_mixed, gate):
    frames, _, near, channels = moved.shape
    shapes = (jax.ShapeDtypeStruct((frames, 2, near, channels), jnp.bfloat16),)
    shapes += (jax.ShapeDtypeStruct((1, channels), jnp.float32),) * terms
    return pl.pallas_call(
        kernel,
        out_shape=shapes,
        in_specs=[pl.BlockSpec(memory_space=pltpu.SMEM)] + in_vmem(3),
        out_specs=tuple(in_vmem(len(shapes))),
        cost_estimate=attention_cost(frames * near, channels),
        compiler_params=pltpu.CompilerParams(vmem_limit_bytes=VMEM_BYTES),
        name=name,
    )(count, moved, grad_mixed, gate)


def space_attention(count, query, key, value, grad_mixed, gate):
    tokens, channels = query.shape
    wide = jax.ShapeDtypeStruct((tokens, channels), jnp.float32)
    return pl.pallas_call(
        space_kernel,
        out_shape=(
            jax.ShapeDtypeStruct((tokens, channels), jnp.bfloat16),
            wide, wide, wide,
            jax.ShapeDtypeStruct((1, channels), jnp.float32),
        ),
        in_specs=[pl.BlockSpec(memory_space=pltpu.SMEM)] + in_vmem(5),
        out_specs=tuple(in_vmem(5)),
        cost_estimate=attention_cost(tokens, channels),
        compiler_params=pltpu.CompilerParams(vmem_limit_bytes=VMEM_BYTES),
        name="space_attention",
    )(count, query, key, value, grad_mixed, gate)


def combine(local, moved):
    wide = moved.astype(jnp.float32).reshape(local.shape)
    return (local + wide).astype(jnp.bfloat16)


def output_kernel(
    time_ref, moved_ref, space_ref, grad_ref, gate_space_ref, gate_time_ref, weight_ref,
    out_ref, out_grad_ref, mixed_ref,
):
    @pl.when(pl.program_id(0) == 0)
    def _():
        moved = time_ref[...].astype(jnp.float32).reshape(space_ref.shape)
        space = space_ref[...].astype(jnp.float32)
        mixed_ref[...] = (gate_space_ref[...] * space + gate_time_ref[...] * moved).astype(jnp.bfloat16)

    out_ref[...] = contract(mixed_ref[...], weight_ref[...], 1, 0).astype(jnp.bfloat16)
    out_grad_ref[...] = combine(grad_ref[...], moved_ref[...])


def output(returned, space, grad, gate_space, gate_time, weight, block=256):
    owners, _, near, channels = returned.shape
    tokens = owners * near
    whole = pl.BlockSpec((tokens, channels), lambda j: (0, 0))
    columns = pl.BlockSpec((tokens, block), lambda j: (0, j))
    gate = pl.BlockSpec((1, channels), lambda j: (0, 0))
    return pl.pallas_call(
        output_kernel,
        grid=(channels // block,),
        out_shape=(jax.ShapeDtypeStruct((tokens, channels), jnp.bfloat16),) * 2,
        in_specs=[
            pl.BlockSpec((owners, 1, near, channels), lambda j: (0, 0, 0, 0)),
            pl.BlockSpec((owners, 1, near, block), lambda j: (0, 1, 0, j)),
            whole, columns, gate, gate,
            pl.BlockSpec((channels, block), lambda j: (0, j)),
        ],
        out_specs=(columns,) * 2,
        scratch_shapes=[pltpu.VMEM((tokens, channels), jnp.bfloat16)],
        compiler_params=pltpu.CompilerParams(vmem_limit_bytes=STREAMING_BYTES),
        cost_estimate=pl.CostEstimate(flops=OUTPUT_FLOPS, bytes_accessed=0, transcendentals=0),
        name="output",
    )(returned, returned, space, grad, gate_space, gate_time, weight)


def add_kernel(moved_ref, key_ref, value_ref, out_key_ref, out_value_ref):
    out_key_ref[...] = combine(key_ref[...], moved_ref[:, 0])
    out_value_ref[...] = combine(value_ref[...], moved_ref[:, 1])


def add_returned(returned, grad_key, grad_value, block=512):
    owners, _, near, channels = returned.shape
    tokens = owners * near
    columns = pl.BlockSpec((tokens, block), lambda j: (0, j))
    return pl.pallas_call(
        add_kernel,
        grid=(channels // block,),
        out_shape=(jax.ShapeDtypeStruct((tokens, channels), jnp.bfloat16),) * 2,
        in_specs=[pl.BlockSpec((owners, 2, near, block), lambda j: (0, 0, 0, j)), columns, columns],
        out_specs=(columns,) * 2,
        compiler_params=pltpu.CompilerParams(vmem_limit_bytes=VMEM_BYTES),
        name="add_returned",
    )(returned, grad_key, grad_value)


def shift(array, axis, by):
    size = lax.axis_size(axis)
    return lax.ppermute(array, axis, [(i, (i + by) % size) for i in range(size)])


def ring_of_four(block, axis):
    half = block.shape[0] // 2
    before, after = shift(block, axis, 1), shift(block, axis, -1)
    across = (shift(before[:half], axis, 1), shift(after[half:], axis, -1))
    return after, across, before


def fetch_rows(out_weight):
    size = lax.axis_size("seq")
    fetched = []
    for slot in range(2):
        pairs = []
        for x, by_core in enumerate(DISTANCES):
            for core, distances in enumerate(by_core):
                first = (2 * x + core) * size
                if distances[slot]:
                    pairs += [(first + (i + distances[slot]) % size, first + i) for i in range(size)]
        fetched.append(lax.ppermute(out_weight, ("x", "core", "seq"), pairs))
    keeps_own = (lax.axis_index("x") == 0) & (lax.axis_index("core") == 0)
    return jnp.stack([jnp.where(keeps_own, out_weight, fetched[0]), fetched[1]])


def weight_kernel(place_ref, *refs):
    *block_refs, out_ref = refs
    number = 0
    for block_ref in block_refs:
        for row in range(block_ref.shape[0]):
            for slot in range(2):
                out_ref[place_ref[number]] = block_ref[row, slot]
                number += 1


def whole_weight(fetched):
    rows, channels = fetched.shape[1:]
    seq = lax.axis_size("seq")
    along_y = jnp.stack([fetched] + [shift(fetched, "fsdp", -by) for by in range(1, 4)])
    after, across, before = ring_of_four(along_y, "x")
    arrays, places = [], []
    distances = jnp.array(DISTANCES, jnp.int32)
    at_x, at_core, at_y, at_seq = (lax.axis_index(axis) for axis in ("x", "core", "fsdp", "seq"))
    for array, by_x, first in (
        (along_y, 0, 0), (after, 1, 0), (across[0], 2, 0), (across[1], 2, 2), (before, 3, 0),
    ):
        for other in range(2):
            arrays.append(shift(array, "core", 1) if other else array)
            core = (at_core + other) % 2
            from_seq = (at_seq + distances[(at_x + by_x) % 4, core]) % seq
            from_y = (at_y + first + jnp.arange(array.shape[0])) % 4
            places.append((from_y[:, None] * seq + from_seq[None, :]).reshape(-1))
    size = 2 * channels * channels
    whole = pl.pallas_call(
        weight_kernel,
        out_shape=jax.ShapeDtypeStruct((4 * seq, rows, channels), jnp.bfloat16),
        in_specs=[pl.BlockSpec(memory_space=pltpu.SMEM)] + in_vmem(len(arrays)),
        out_specs=in_vmem(1)[0],
        cost_estimate=pl.CostEstimate(flops=WEIGHT_FLOPS, bytes_accessed=size, transcendentals=0),
        compiler_params=pltpu.CompilerParams(vmem_limit_bytes=VMEM_BYTES),
        name="weight_in_place",
    )(jnp.concatenate(places).astype(jnp.int32), *arrays)
    return whole.reshape(channels, channels)


def all_sum(array, axis):
    return jnp.sum(lax.all_gather(array, axis, axis=0, tiled=True), axis=0, keepdims=True)


def frame_pair(array):
    size, chips = lax.axis_size("seq"), lax.axis_size("x")
    fetched = []
    for step in range(2):
        pairs = []
        for group in range(2 * chips):
            by = 2 * group + step
            if by:
                pairs += [(group * size + i, group * size + (i ^ by)) for i in range(size)]
        fetched.append(lax.ppermute(array, ("x", "core", "seq"), pairs))
    own = jnp.where((lax.axis_index("x") == 0) & (lax.axis_index("core") == 0), array, 0.0)
    return (fetched[0] + own) + fetched[1]


def group_sum(total):
    terms = list(lax.all_gather(total, ("x", "core"), axis=0, tiled=True))
    while len(terms) > 1:
        terms = [left + right for left, right in zip(terms[::2], terms[1::2])]
    return all_sum(terms[0][None], "fsdp")[0]


def on_device(
    query_states,
    key_states,
    value_states,
    out_weight,
    gate_space,
    gate_time,
    upstream,
    frame_count,
    pos_count,
):
    _, frames_here, positions, channels = query_states.shape
    owners = lax.axis_size("seq")
    near = positions // owners
    gate_space, gate_time = gate_space.reshape(1, channels), gate_time.reshape(1, channels)
    query, key, value, flat_up = (
        array.reshape(positions, channels)
        for array in (query_states, key_states, value_states, upstream)
    )

    def exchange(array):
        return lax.all_to_all(array, "seq", split_axis=0, concat_axis=0, tiled=True)

    fetched = fetch_rows(out_weight)
    sent = jnp.stack(
        [array.reshape(owners, near, channels) for array in (query, key, value, flat_up)], axis=1
    )
    moved = exchange(sent)

    weight = whole_weight(fetched)

    def project(array):
        return jnp.einsum("td,nd->tn", array, weight, preferred_element_type=jnp.float32)

    space, grad_query, grad_key, grad_value, part_space = space_attention(
        pos_count, query, key, value, project(flat_up), gate_space
    )
    moved, part_space = lax.optimization_barrier((moved, part_space))
    there = project(moved[:, 3].reshape(positions, channels))
    early, part_time = time_attention(
        time_values_kernel, "time_attention", 1, frame_count, moved, there, gate_time
    )
    (late,) = time_attention(time_scores_kernel, "time_scores", 0, frame_count, moved, there, gate_time)
    early = exchange(early)

    parts = jnp.concatenate([part_space, part_time], axis=1)
    parts = all_sum(parts, ("x", "core"))
    early, late, _ = lax.optimization_barrier((early, late, parts))
    parts = frame_pair(parts)
    late = exchange(late)
    tokens = lax.axis_size("x") * lax.axis_size("core") * lax.axis_size("fsdp") * owners * frames_here * positions
    totals = group_sum(parts) / math.sqrt(tokens)

    results = output(early, space, grad_value, gate_space, gate_time, weight)
    results = (results[0], *add_returned(late, grad_query, grad_key), results[1])
    shaped = tuple(array.reshape(query_states.shape) for array in results)
    return shaped + (totals[:channels], totals[channels:])


def solution(mesh):
    chips = mesh.shape["dp"] // 2
    split = Mesh(
        mesh.devices.reshape(chips, 2, mesh.shape["fsdp"], mesh.shape["seq"]),
        ("x", "core", "fsdp", "seq"),
    )
    clips = ("x", "core", "fsdp")
    states = P(clips, "seq", None, None)
    return jax.shard_map(
        on_device,
        mesh=split,
        in_specs=(states, states, states, P(("fsdp", "seq"), None), P(), P(), states, P(clips), P(clips)),
        out_specs=(states, states, states, states, P(), P()),
        check_vma=False,
    )
```

```python
import functools
import math

import jax
import jax.numpy as jnp
from jax import lax
from jax.experimental import pallas as pl
from jax.experimental.pallas import tpu as pltpu
from jax.sharding import Mesh, PartitionSpec as P

HEAD = 128
NEGATIVE = -1e30
VMEM_BYTES = 20 * 1024 * 1024
STREAMING_BYTES = 60 * 1024 * 1024
WEIGHT_FLOPS = 36_800_000_000
OUTPUT_FLOPS = 16_100_000_000
DISTANCES = (((0, 8), (4, -4)), ((1, -1), (7, -7)), ((2, -2), (6, -6)), ((3, -3), (5, -5)))


def contract(left, right, left_dim, right_dim):
    return lax.dot_general(
        left,
        right,
        (((left_dim,), (right_dim,)), ((), ())),
        preferred_element_type=jnp.float32,
    )


def head_probs(query, key, keep):
    scores = jnp.where(keep, contract(key, query, 1, 1) * HEAD ** (-0.5), NEGATIVE)
    raised = jnp.exp(scores - jnp.max(scores, axis=0, keepdims=True))
    return raised / jnp.sum(raised, axis=0, keepdims=True)


def head_values(probs, value, grad_mixed, gate):
    rounded = probs.astype(jnp.bfloat16)
    result = contract(rounded, value, 0, 0).astype(jnp.bfloat16)
    part = jnp.sum(grad_mixed * result.astype(jnp.float32), axis=0, keepdims=True)
    return result, contract(rounded, (gate * grad_mixed).astype(jnp.bfloat16), 1, 0), part


def head_scores(probs, query, key, value, grad_mixed, gate):
    grad_probs = contract(value, (gate * grad_mixed).astype(jnp.bfloat16), 1, 1)
    inner = jnp.sum(probs * grad_probs, axis=0, keepdims=True)
    grad_scores = (probs * (grad_probs - inner) * HEAD ** (-0.5)).astype(jnp.bfloat16)
    return contract(grad_scores, key, 0, 0), contract(grad_scores, query, 1, 0)


def head_gradients(query, key, value, grad_mixed, gate, keep):
    probs = head_probs(query, key, keep)
    result, grad_value, part = head_values(probs, value, grad_mixed, gate)
    grad_query, grad_key = head_scores(probs, query, key, value, grad_mixed, gate)
    return result, grad_query, grad_key, grad_value, part


def time_heads(count_ref, moved_ref, mixed_ref, gate_ref):
    frames, _, near, channels = moved_ref.shape
    tokens = frames * near
    key_at = lax.broadcasted_iota(jnp.int32, (tokens, tokens), 0)
    query_at = lax.broadcasted_iota(jnp.int32, (tokens, tokens), 1)
    keep = (key_at % near == query_at % near) & (key_at < count_ref[0] * near)
    for head in range(channels // HEAD):
        lanes = slice(head * HEAD, (head + 1) * HEAD)
        arrays = [
            moved_ref[:, which, :, lanes].astype(jnp.float32).reshape(tokens, HEAD).astype(jnp.bfloat16)
            for which in range(3)
        ]
        probs = head_probs(arrays[0], arrays[1], keep)
        yield lanes, probs, arrays, mixed_ref[:, lanes], gate_ref[:, lanes]


def put_by_frame(target, which, lanes, array):
    frames, _, near, _ = target.shape
    wide = array.astype(jnp.float32).reshape(frames, near, HEAD)
    target[:, which, :, lanes] = wide.astype(jnp.bfloat16)


def time_values_kernel(count_ref, moved_ref, mixed_ref, gate_ref, out_ref, part_ref):
    for lanes, probs, arrays, mixed, gate in time_heads(count_ref, moved_ref, mixed_ref, gate_ref):
        result, grad_value, part = head_values(probs, arrays[2], mixed, gate)
        part_ref[:, lanes] = part
        put_by_frame(out_ref, 0, lanes, result)
        put_by_frame(out_ref, 1, lanes, grad_value)


def time_scores_kernel(count_ref, moved_ref, mixed_ref, gate_ref, out_ref):
    for lanes, probs, arrays, mixed, gate in time_heads(count_ref, moved_ref, mixed_ref, gate_ref):
        for which, array in enumerate(head_scores(probs, *arrays, mixed, gate)):
            put_by_frame(out_ref, which, lanes, array)


def space_kernel(
    count_ref, query_ref, key_ref, value_ref, mixed_ref, gate_ref,
    out_ref, grad_query_ref, grad_key_ref, grad_value_ref, part_ref,
):
    tokens, channels = query_ref.shape
    keep = lax.broadcasted_iota(jnp.int32, (tokens, tokens), 0) < count_ref[0]
    for head in range(channels // HEAD):
        lanes = slice(head * HEAD, (head + 1) * HEAD)
        result, grad_query, grad_key, grad_value, part = head_gradients(
            query_ref[:, lanes], key_ref[:, lanes], value_ref[:, lanes],
            mixed_ref[:, lanes], gate_ref[:, lanes], keep,
        )
        out_ref[:, lanes] = result
        grad_query_ref[:, lanes] = grad_query
        grad_key_ref[:, lanes] = grad_key
        grad_value_ref[:, lanes] = grad_value
        part_ref[:, lanes] = part


def in_vmem(count):
    return [pl.BlockSpec(memory_space=pltpu.VMEM)] * count


def attention_cost(tokens, channels):
    return pl.CostEstimate(
        flops=12 * tokens * tokens * channels,
        bytes_accessed=16 * tokens * channels,
        transcendentals=tokens * tokens * channels // HEAD,
    )


def time_attention(kernel, name, terms, count, moved, grad_mixed, gate):
    frames, _, near, channels = moved.shape
    shapes = (jax.ShapeDtypeStruct((frames, 2, near, channels), jnp.bfloat16),)
    shapes += (jax.ShapeDtypeStruct((1, channels), jnp.float32),) * terms
    return pl.pallas_call(
        kernel,
        out_shape=shapes,
        in_specs=[pl.BlockSpec(memory_space=pltpu.SMEM)] + in_vmem(3),
        out_specs=tuple(in_vmem(len(shapes))),
        cost_estimate=attention_cost(frames * near, channels),
        compiler_params=pltpu.CompilerParams(vmem_limit_bytes=VMEM_BYTES),
        name=name,
    )(count, moved, grad_mixed, gate)


def space_attention(count, query, key, value, grad_mixed, gate):
    tokens, channels = query.shape
    wide = jax.ShapeDtypeStruct((tokens, channels), jnp.float32)
    return pl.pallas_call(
        space_kernel,
        out_shape=(
            jax.ShapeDtypeStruct((tokens, channels), jnp.bfloat16),
            wide, wide, wide,
            jax.ShapeDtypeStruct((1, channels), jnp.float32),
        ),
        in_specs=[pl.BlockSpec(memory_space=pltpu.SMEM)] + in_vmem(5),
        out_specs=tuple(in_vmem(5)),
        cost_estimate=attention_cost(tokens, channels),
        compiler_params=pltpu.CompilerParams(vmem_limit_bytes=VMEM_BYTES),
        name="space_attention",
    )(count, query, key, value, grad_mixed, gate)


def combine(local, moved):
    wide = moved.astype(jnp.float32).reshape(local.shape)
    return (local + wide).astype(jnp.bfloat16)


def output_kernel(
    time_ref, moved_ref, space_ref, grad_ref, gate_space_ref, gate_time_ref, weight_ref,
    out_ref, out_grad_ref, mixed_ref,
):
    @pl.when(pl.program_id(0) == 0)
    def _():
        moved = time_ref[...].astype(jnp.float32).reshape(space_ref.shape)
        space = space_ref[...].astype(jnp.float32)
        mixed_ref[...] = (gate_space_ref[...] * space + gate_time_ref[...] * moved).astype(jnp.bfloat16)

    out_ref[...] = contract(mixed_ref[...], weight_ref[...], 1, 0).astype(jnp.bfloat16)
    out_grad_ref[...] = combine(grad_ref[...], moved_ref[...])


def output(returned, space, grad, gate_space, gate_time, weight, block=512):
    owners, _, near, channels = returned.shape
    tokens = owners * near
    whole = pl.BlockSpec((tokens, channels), lambda j: (0, 0))
    columns = pl.BlockSpec((tokens, block), lambda j: (0, j))
    gate = pl.BlockSpec((1, channels), lambda j: (0, 0))
    return pl.pallas_call(
        output_kernel,
        grid=(channels // block,),
        out_shape=(jax.ShapeDtypeStruct((tokens, channels), jnp.bfloat16),) * 2,
        in_specs=[
            pl.BlockSpec((owners, 1, near, channels), lambda j: (0, 0, 0, 0)),
            pl.BlockSpec((owners, 1, near, block), lambda j: (0, 1, 0, j)),
            whole, columns, gate, gate,
            pl.BlockSpec((channels, block), lambda j: (0, j)),
        ],
        out_specs=(columns,) * 2,
        scratch_shapes=[pltpu.VMEM((tokens, channels), jnp.bfloat16)],
        compiler_params=pltpu.CompilerParams(vmem_limit_bytes=STREAMING_BYTES),
        cost_estimate=pl.CostEstimate(flops=OUTPUT_FLOPS, bytes_accessed=0, transcendentals=0),
        name="output",
    )(returned, returned, space, grad, gate_space, gate_time, weight)


def add_kernel(moved_ref, key_ref, value_ref, out_key_ref, out_value_ref):
    out_key_ref[...] = combine(key_ref[...], moved_ref[:, 0])
    out_value_ref[...] = combine(value_ref[...], moved_ref[:, 1])


def add_returned(returned, grad_key, grad_value, block=512):
    owners, _, near, channels = returned.shape
    tokens = owners * near
    columns = pl.BlockSpec((tokens, block), lambda j: (0, j))
    return pl.pallas_call(
        add_kernel,
        grid=(channels // block,),
        out_shape=(jax.ShapeDtypeStruct((tokens, channels), jnp.bfloat16),) * 2,
        in_specs=[pl.BlockSpec((owners, 2, near, block), lambda j: (0, 0, 0, j)), columns, columns],
        out_specs=(columns,) * 2,
        compiler_params=pltpu.CompilerParams(vmem_limit_bytes=VMEM_BYTES),
        name="add_returned",
    )(returned, grad_key, grad_value)


def shift(array, axis, by):
    size = lax.axis_size(axis)
    return lax.ppermute(array, axis, [(i, (i + by) % size) for i in range(size)])


def ring_of_four(block, axis):
    half = block.shape[0] // 2
    before, after = shift(block, axis, 1), shift(block, axis, -1)
    across = (shift(before[:half], axis, 1), shift(after[half:], axis, -1))
    return after, across, before


def fetch_rows(out_weight):
    size = lax.axis_size("seq")
    fetched = []
    for slot in range(2):
        pairs = []
        for x, by_core in enumerate(DISTANCES):
            for core, distances in enumerate(by_core):
                first = (2 * x + core) * size
                if distances[slot]:
                    pairs += [(first + (i + distances[slot]) % size, first + i) for i in range(size)]
        fetched.append(lax.ppermute(out_weight, ("x", "core", "seq"), pairs))
    keeps_own = (lax.axis_index("x") == 0) & (lax.axis_index("core") == 0)
    return jnp.stack([jnp.where(keeps_own, out_weight, fetched[0]), fetched[1]])


def weight_kernel(place_ref, *refs):
    *block_refs, out_ref = refs
    number = 0
    for block_ref in block_refs:
        for row in range(block_ref.shape[0]):
            for slot in range(2):
                out_ref[place_ref[number]] = block_ref[row, slot]
                number += 1


def whole_weight(fetched):
    rows, channels = fetched.shape[1:]
    seq = lax.axis_size("seq")
    along_y = jnp.stack([fetched] + [shift(fetched, "fsdp", -by) for by in range(1, 4)])
    after, across, before = ring_of_four(along_y, "x")
    arrays, places = [], []
    distances = jnp.array(DISTANCES, jnp.int32)
    at_x, at_core, at_y, at_seq = (lax.axis_index(axis) for axis in ("x", "core", "fsdp", "seq"))
    for array, by_x, first in (
        (along_y, 0, 0), (after, 1, 0), (across[0], 2, 0), (across[1], 2, 2), (before, 3, 0),
    ):
        for other in range(2):
            arrays.append(shift(array, "core", 1) if other else array)
            core = (at_core + other) % 2
            from_seq = (at_seq + distances[(at_x + by_x) % 4, core]) % seq
            from_y = (at_y + first + jnp.arange(array.shape[0])) % 4
            places.append((from_y[:, None] * seq + from_seq[None, :]).reshape(-1))
    size = 2 * channels * channels
    whole = pl.pallas_call(
        weight_kernel,
        out_shape=jax.ShapeDtypeStruct((4 * seq, rows, channels), jnp.bfloat16),
        in_specs=[pl.BlockSpec(memory_space=pltpu.SMEM)] + in_vmem(len(arrays)),
        out_specs=in_vmem(1)[0],
        cost_estimate=pl.CostEstimate(flops=WEIGHT_FLOPS, bytes_accessed=size, transcendentals=0),
        compiler_params=pltpu.CompilerParams(vmem_limit_bytes=VMEM_BYTES),
        name="weight_in_place",
    )(jnp.concatenate(places).astype(jnp.int32), *arrays)
    return whole.reshape(channels, channels)


def all_sum(array, axis):
    return jnp.sum(lax.all_gather(array, axis, axis=0, tiled=True), axis=0, keepdims=True)


def frame_pair(array):
    size, chips = lax.axis_size("seq"), lax.axis_size("x")
    fetched = []
    for step in range(2):
        pairs = []
        for group in range(2 * chips):
            by = 2 * group + step
            if by:
                pairs += [(group * size + i, group * size + (i ^ by)) for i in range(size)]
        fetched.append(lax.ppermute(array, ("x", "core", "seq"), pairs))
    own = jnp.where((lax.axis_index("x") == 0) & (lax.axis_index("core") == 0), array, 0.0)
    return (fetched[0] + own) + fetched[1]


def group_sum(total):
    terms = list(lax.all_gather(total, ("x", "core"), axis=0, tiled=True))
    while len(terms) > 1:
        terms = [left + right for left, right in zip(terms[::2], terms[1::2])]
    return all_sum(terms[0][None], "fsdp")[0]


def on_device(
    query_states,
    key_states,
    value_states,
    out_weight,
    gate_space,
    gate_time,
    upstream,
    frame_count,
    pos_count,
):
    _, frames_here, positions, channels = query_states.shape
    owners = lax.axis_size("seq")
    near = positions // owners
    gate_space, gate_time = gate_space.reshape(1, channels), gate_time.reshape(1, channels)
    query, key, value, flat_up = (
        array.reshape(positions, channels)
        for array in (query_states, key_states, value_states, upstream)
    )

    def exchange(array):
        return lax.all_to_all(array, "seq", split_axis=0, concat_axis=0, tiled=True)

    fetched = fetch_rows(out_weight)
    sent = jnp.stack(
        [array.reshape(owners, near, channels) for array in (query, key, value, flat_up)], axis=1
    )
    moved = exchange(sent)

    weight = whole_weight(fetched)

    def project(array):
        return jnp.einsum("td,nd->tn", array, weight, preferred_element_type=jnp.float32)

    space, grad_query, grad_key, grad_value, part_space = space_attention(
        pos_count, query, key, value, project(flat_up), gate_space
    )
    moved, part_space = lax.optimization_barrier((moved, part_space))
    there = project(moved[:, 3].reshape(positions, channels))
    early, part_time = time_attention(
        time_values_kernel, "time_attention", 1, frame_count, moved, there, gate_time
    )
    (late,) = time_attention(time_scores_kernel, "time_scores", 0, frame_count, moved, there, gate_time)
    early = exchange(early)

    parts = jnp.concatenate([part_space, part_time], axis=1)
    parts = all_sum(parts, ("x", "core"))
    early, late, _ = lax.optimization_barrier((early, late, parts))
    parts = frame_pair(parts)
    late = exchange(late)
    tokens = lax.axis_size("x") * lax.axis_size("core") * lax.axis_size("fsdp") * owners * frames_here * positions
    totals = group_sum(parts) / math.sqrt(tokens)

    results = output(early, space, grad_value, gate_space, gate_time, weight)
    results = (results[0], *add_returned(late, grad_query, grad_key), results[1])
    shaped = tuple(array.reshape(query_states.shape) for array in results)
    return shaped + (totals[:channels], totals[channels:])


def solution(mesh):
    chips = mesh.shape["dp"] // 2
    split = Mesh(
        mesh.devices.reshape(chips, 2, mesh.shape["fsdp"], mesh.shape["seq"]),
        ("x", "core", "fsdp", "seq"),
    )
    clips = ("x", "core", "fsdp")
    states = P(clips, "seq", None, None)
    return jax.shard_map(
        on_device,
        mesh=split,
        in_specs=(states, states, states, P(("fsdp", "seq"), None), P(), P(), states, P(clips), P(clips)),
        out_specs=(states, states, states, states, P(), P()),
        check_vma=False,
    )
```
